32 devices in a mesh: dp: 4 (over x, core), tensor: 8 (over z, y).
Axes of the slice: x: 2, y: 2, z: 4, core: 2. Of those that a mesh axis runs over, the one named last changes fastest.
Arguments:
- activations: bfloat16 [2048, 8192], P('dp', 'tensor'), may hold values from -6 to 6
- left_factor: bfloat16 [1024, 8192], P(None, 'tensor'), may hold values from -0.0625 to 0.0625
- right_factor: bfloat16 [1024, 16384], P(None, 'tensor'), may hold values from -0.1875 to 0.1875
- out_grad: bfloat16 [2048, 16384], P('dp', 'tensor'), may hold values from -6 to 6
Outputs:
- input_grad: bfloat16 [2048, 8192], P('dp', 'tensor')
- left_grad: float32 [1024, 8192], P('dp', 'tensor')
- right_grad: float32 [1024, 16384], P('dp', 'tensor')
The draws below stay inside these ranges and needn't reach their ends.
All inputs are finite; a program needn't handle non-finite values.
Results may differ from the reference program's by a relative error of at most 0.0049.
Values may be sent and summed in bfloat16 or wider, within the bound.
No kernel may reach another device: no remote copies, remote signals or barrier semaphores. Data moves between devices by JAX's collectives and lax.ppermute only.
A program may use at most 64 MiB of HBM per device.

```python
import math
import jax
import jax.numpy as jnp
from jax import lax

D = 8192
FF = 16384
R = 1024
TOKENS = 2048


def levels(rng, extent, pieces, smallest, largest):
    def one(axis_at, shards_of):
        heights = jax.random.uniform(jax.random.fold_in(jax.random.fold_in(rng, 6), axis_at), (shards_of,), jnp.float32, smallest / len(pieces), largest / len(pieces))
        return jnp.repeat(jnp.exp(heights), extent[axis_at] // shards_of).reshape((-1,) + (1,) * (len(extent) - axis_at - 1))

    loudness = one(*pieces[0])
    for cut in pieces[1:]:
        loudness = loudness * one(*cut)
    return loudness


def bell_draw(own_key, shape, deviation, bound, split=(), dtype=jnp.bfloat16):
    level = levels(own_key, shape, split, -0.22, 0.18) if split else 1.0
    entries = jax.random.normal(own_key, shape, jnp.float32) * deviation * level
    return jnp.minimum(jnp.maximum(entries, -bound), bound).astype(dtype)


def setup_inputs(seed: int = 0) -> dict:
    key_of = jax.random.split(jax.random.key(seed), 5)
    return {
        "activations": bell_draw(key_of[0], (TOKENS, D), 1.0, 6.0, ((0, 4), (1, 8))),
        "left_factor": bell_draw(key_of[1], (R, D), D ** -0.5, 0.0625, ((1, 8),)),
        "right_factor": bell_draw(key_of[2], (R, FF), R ** -0.5, 0.1875, ((1, 8),)),
        "out_grad": bell_draw(key_of[3], (TOKENS, FF), 1.0, 6.0, ((0, 4), (1, 8))),
    }


def reference(activations, left_factor, right_factor, out_grad):
    dims = (((1,), (1,)), ((), ()))
    latent = lax.dot_general(activations, left_factor, dims, preferred_element_type=jnp.float32).astype(jnp.bfloat16)
    latent_grad = lax.dot_general(out_grad, right_factor, dims, preferred_element_type=jnp.float32).astype(jnp.bfloat16)
    input_grad = jnp.dot(latent_grad, left_factor, preferred_element_type=jnp.float32).astype(jnp.bfloat16)
    scale = 1.0 / math.sqrt(TOKENS)
    rows = (((0,), (0,)), ((), ()))
    right_grad = lax.dot_general(latent, out_grad, rows, preferred_element_type=jnp.float32) * scale
    left_grad = lax.dot_general(latent_grad, activations, rows, preferred_element_type=jnp.float32) * scale
    return (input_grad, left_grad, right_grad)
```

```python
import math

import jax
import jax.numpy as jnp
from jax import lax
from jax.sharding import PartitionSpec as P

CHUNKS = 1


def rows_by_rows(first, second):
    return lax.dot_general(
        first, second, (((0,), (0,)), ((), ())), preferred_element_type=jnp.float32
    )


def cols_by_cols(first, second):
    return lax.dot_general(
        first, second, (((1,), (1,)), ((), ())), preferred_element_type=jnp.float32
    )


def swap(value, axis, mask):
    size = lax.axis_size(axis)
    return lax.ppermute(value, axis, [(i, i ^ mask) for i in range(size)])


def pick(value, index, size, axis=0):
    return lax.dynamic_slice_in_dim(value, index * size, size, axis)


def summed(part, place):
    width = lax.axis_size("tensor")
    half = part.shape[0] // 2
    low, high = place % 2, place // 2
    sent = swap(pick(part, 1 - low, half).astype(jnp.bfloat16), "tensor", 1)
    total = pick(part, low, half) + sent.astype(jnp.float32)
    share = half // (width // 2)
    mine = pick(total, high, share)
    for step in range(1, width // 2):
        piece = pick(total, high ^ step, share).astype(jnp.bfloat16)
        mine = mine + swap(piece, "tensor", 2 * step).astype(jnp.float32)
    return mine.astype(jnp.bfloat16)


def gathered(mine, place):
    width = lax.axis_size("tensor")
    share = mine.shape[0]
    low, high = place % 2, place // 2
    half = share * (width // 2)
    whole = jnp.zeros((half,) + mine.shape[1:], mine.dtype)
    for step in range(width // 2):
        piece = swap(mine, "tensor", 2 * step) if step else mine
        whole = lax.dynamic_update_slice_in_dim(whole, piece, (high ^ step) * share, 0)
    other = swap(whole, "tensor", 1)
    return jnp.where(
        low == 0, jnp.concatenate([whole, other]), jnp.concatenate([other, whole])
    )


def owned(part, group):
    owners = part.shape[0]
    mine = lax.dynamic_index_in_dim(part, group, 0, False)
    for step in range(1, owners):
        block = lax.dynamic_index_in_dim(part, group ^ step, 0, False)
        mine = mine + swap(block.astype(jnp.bfloat16), "dp", 2 * step).astype(jnp.float32)
    return mine


def shards(activations, left_factor, right_factor, out_grad):
    groups = lax.axis_size("dp")
    tokens = activations.shape[0]
    rank = left_factor.shape[0]
    owners = groups // 2
    rows = rank // groups
    scale = 1.0 / math.sqrt(tokens * groups)
    place = lax.axis_index("tensor")
    spot = lax.axis_index("dp")
    core, group = spot % 2, spot // 2

    def of_core(factor, which):
        blocks = factor.reshape(owners, 2, rows, factor.shape[1])
        return lax.dynamic_index_in_dim(blocks, which, 1, False)

    acts = jnp.concatenate([activations, swap(activations, "dp", 1)])
    grads = jnp.concatenate([out_grad, swap(out_grad, "dp", 1)])
    left = of_core(left_factor, core)
    left_other = of_core(left_factor, 1 - core)
    right = of_core(right_factor, core)

    step = rows // CHUNKS
    spans = [slice(i * step, (i + 1) * step) for i in range(CHUNKS)]

    def part_of(values, factor, span):
        return cols_by_cols(values, factor[:, span].reshape(owners * step, factor.shape[2]))

    latents = [gathered(summed(part_of(acts, left, s), place), place) for s in spans]
    latent_grads = [gathered(summed(part_of(grads, right, s), place), place) for s in spans]

    def weight_grad(pieces, values):
        done = []
        for piece in pieces:
            part = rows_by_rows(piece, values).reshape(owners, step, values.shape[1])
            done.append(owned(part, group) * scale)
        return jnp.concatenate(done)

    right_grad = weight_grad(latents, grads)
    left_grad = weight_grad(latent_grads, acts)

    def flat(factor, span):
        return factor[:, span].reshape(owners * step, factor.shape[2])

    total = 0.0
    for piece, span in zip(latent_grads, spans, strict=True):
        other = swap(piece[tokens:], "dp", 1)
        total = total + jnp.dot(
            piece[:tokens], flat(left, span), preferred_element_type=jnp.float32
        )
        total = total + jnp.dot(other, flat(left_other, span), preferred_element_type=jnp.float32)
    return total.astype(jnp.bfloat16), left_grad, right_grad


def solution(mesh):
    placed = (P("dp", "tensor"), P(None, "tensor"), P(None, "tensor"), P("dp", "tensor"))
    return jax.shard_map(
        shards,
        mesh=mesh,
        in_specs=placed,
        out_specs=(P("dp", "tensor"), P("dp", "tensor"), P("dp", "tensor")),
        check_vma=False,
    )
```

```python
import functools
import math

import jax
import jax.numpy as jnp
from jax import lax
from jax.experimental import pallas as pl
from jax.experimental.pallas import tpu as pltpu
from jax.sharding import PartitionSpec as P

CHUNKS = 2
NAMES = {"G": "latent_grad", "L": "latent", "x": "far", "c": "core"}
ORDER = (
    "G0S", "G1S", "LS", "own", "GK", "G0near", "LK", "G1near", "G0far", "L0near", "G1far",
    "L1near", "L0far", "G0last", "G1last", "L1far", "G0join", "L0last", "G1join", "L0stack",
    "L1last", "G0halves", "L0join", "og", "L1stack", "G1halves", "G0left", "L1join", "G1left",
    "input", "Lrn", "Lrf", "final",
)
HALVES = {"G": (True, True), "L": (True, False)}
BF16 = jnp.bfloat16
F32 = jnp.float32
MIB = 1 << 20
COLS = (((1,), (1,)), ((), ()))
ROWS = (((0,), (0,)), ((), ()))


def dot(first, second, dims):
    return lax.dot_general(first, second, dims, preferred_element_type=F32)


def cost(flops, *arrays):
    sizes = []
    for array in arrays:
        shape, dtype = array if isinstance(array, tuple) else (array.shape, array.dtype)
        sizes.append(math.prod(shape) * jnp.dtype(dtype).itemsize)
    return pl.CostEstimate(flops=flops, bytes_accessed=sum(sizes), transcendentals=0)


def whole_call(kernel, where, values, outs, scratch=(), flops=0):
    return pl.pallas_call(
        kernel,
        out_shape=[jax.ShapeDtypeStruct(s, t) for s, t in outs],
        in_specs=[pl.BlockSpec(memory_space=pltpu.SMEM)]
        + [pl.BlockSpec(memory_space=pltpu.VMEM)] * len(values),
        out_specs=[pl.BlockSpec(memory_space=pltpu.VMEM)] * len(outs),
        scratch_shapes=list(scratch),
        compiler_params=pltpu.CompilerParams(vmem_limit_bytes=24 * MIB),
        cost_estimate=cost(flops, *values, *outs),
    )(where, *values)


def swap(value, axis, mask):
    size = lax.axis_size(axis)
    return lax.ppermute(value, axis, [(i, i ^ mask) for i in range(size)])


def tied(value, run):
    return lax.optimization_barrier((value, run.last))[0]


class InOrder:
    def __init__(self):
        self.last = ()

    def __call__(self, step, *values):
        values, _ = lax.optimization_barrier((values, self.last))
        result = step(*values)
        self.last = result
        return result


def product_kernel(chunks, where, *refs):
    values, factor, outs = refs[:-chunks - 1], refs[-chunks - 1], refs[-chunks:]
    count, width = outs[0].shape[0], outs[0].shape[2]
    flat = factor[...].reshape(count * chunks * width, factor.shape[-1])
    rows = values[0].shape[0]
    for i, value in enumerate(values):
        result = dot(value[...], flat, COLS)
        for j in range(count):
            for c in range(chunks):
                lane = (j * chunks + c) * width
                part = result[:, lane : lane + width]
                outs[c][j, i * rows : (i + 1) * rows, :] = part.astype(outs[c].dtype)


def products(where, which, values, factor, block, place, dtype, batch, chunks, limit):
    rows, depth = values[0].shape
    half = rows // 2
    width = block[-2]
    count = math.prod(block[:-3])
    total = half * len(values)

    def half_of(i, where):
        return (where[0] if which else 1 - where[0], 0)

    return pl.pallas_call(
        functools.partial(product_kernel, chunks),
        out_shape=[jax.ShapeDtypeStruct((count, total, width), dtype)] * chunks,
        grid_spec=pltpu.PrefetchScalarGridSpec(
            num_scalar_prefetch=1,
            grid=(count // batch,),
            in_specs=[pl.BlockSpec((half, depth), half_of)] * len(values)
            + [pl.BlockSpec((batch,) + block[1:], place)],
            out_specs=[pl.BlockSpec((batch, total, width), lambda i, where: (i, 0, 0))] * chunks,
        ),
        compiler_params=pltpu.CompilerParams(vmem_limit_bytes=limit * MIB),
        cost_estimate=cost(
            2 * total * depth * count * chunks * width,
            *values,
            ((count, chunks, width, depth), BF16),
        ),
    )(where, *values, factor)


def split_kernel(where, kept, sent, mine, away):
    rows = mine.shape[1]
    if rows == kept.shape[1]:
        total = kept[...] + sent[...].astype(F32)
        mine[...] = total
        away[...] = total.astype(BF16)
        return
    for out, at in ((mine, where[4]), (away, 1 - where[4])):
        span = pl.ds(pl.multiple_of(at * rows, rows), rows)
        out[...] = (kept[:, span, :] + sent[:, span, :].astype(F32)).astype(out.dtype)


def split(where, parts, kept, sent):
    count, rows, width = kept.shape
    shape = (count, rows // parts, width)
    return whole_call(split_kernel, where, [kept, sent], [(shape, F32), (shape, BF16)])


def added_kernel(where, mine, other, out, away):
    total = mine[...] + other[...].astype(F32)
    out[...] = total
    away[...] = total.astype(BF16)


def added(where, mine, other):
    return whole_call(
        added_kernel, where, [mine, other], [(mine.shape, F32), (mine.shape, BF16)]
    )


def summed_kernel(where, mine, other, out):
    out[...] = (mine[...] + other[...].astype(F32)).astype(BF16)


def summed(where, mine, other):
    return whole_call(summed_kernel, where, [mine, other], [(mine.shape, BF16)])[0]


def summed_by_owner_kernel(where, mine, other, *outs):
    for step, out in enumerate(outs):
        at = where[3] ^ step
        out[...] = (mine[at] + other[at].astype(F32)).astype(BF16)


def summed_by_owner(where, mine, other):
    owners = mine.shape[0]
    return whole_call(
        summed_by_owner_kernel, where, [mine, other], [(mine.shape[1:], BF16)] * owners
    )


def stacked_kernel(where, *refs):
    *pieces, out = refs
    for i, piece in enumerate(pieces):
        out[i] = piece[...]


def stacked(where, *pieces):
    return whole_call(
        stacked_kernel, where, list(pieces), [((len(pieces),) + pieces[0].shape, BF16)]
    )[0]


def joined_kernel(where, mine, other, out):
    rows = mine.shape[1]
    for part, at in ((mine, where[4]), (other, 1 - where[4])):
        out[:, pl.ds(pl.multiple_of(at * rows, rows), rows), :] = part[...]


def joined(where, mine, other):
    count, rows, width = mine.shape
    return whole_call(joined_kernel, where, [mine, other], [((count, 2 * rows, width), BF16)])[0]


def halves_kernel(owners, where, near, far, out):
    for i, part in enumerate((near, far)):
        for owner in range(owners):
            out[i, owner] = part[owner * 2 + 1 - where[2]]


def halves(where, owners, near, far):
    return whole_call(
        functools.partial(halves_kernel, owners),
        where,
        [near, far],
        [((2, owners) + near.shape[1:], BF16)],
    )[0]


def left_kernel(owners, where, near, far, theirs, acts, acts_other, mine, *rest):
    blocks, (ordered, result) = rest[: owners - 1], rest[owners - 1 :]
    _, share, width = near.shape
    for i, part in enumerate((near, far)):
        low = where[0] if i == 0 else 1 - where[0]
        span = pl.ds(pl.multiple_of(low * share, share), share)
        for owner in range(owners):
            lanes = slice(owner * width, (owner + 1) * width)
            ordered[0, span, lanes] = part[owner * 2 + where[2]]
            ordered[1, span, lanes] = theirs[i, owner]
    result[...] = dot(ordered[0], acts[...], ROWS) + dot(ordered[1], acts_other[...], ROWS)
    for step in range(owners):
        rows = pl.ds(pl.multiple_of((where[3] ^ step) * width, width), width)
        if step:
            blocks[step - 1][...] = result[rows, :].astype(BF16)
        else:
            mine[...] = result[rows, :]


def left_parts(where, owners, near, far, theirs, acts, acts_other):
    width = near.shape[-1]
    tokens, depth = acts.shape
    mine, *blocks = whole_call(
        functools.partial(left_kernel, owners),
        where,
        [near, far, theirs, acts, acts_other],
        [((width, depth), F32)] + [((width, depth), BF16)] * (owners - 1),
        [
            pltpu.VMEM((2, tokens, owners * width), BF16),
            pltpu.VMEM((owners * width, depth), F32),
        ],
        4 * tokens * owners * width * depth,
    )
    return mine, blocks


def input_kernel(count, where, *refs):
    parts, (factor, out, ordered) = refs[: 2 * count], refs[2 * count :]
    groups, share, width = parts[0].shape
    block = out.shape[1]

    @pl.when(pl.program_id(0) == 0)
    def _():
        for chunk in range(count):
            for i in range(2):
                low = where[0] if i == 0 else 1 - where[0]
                span = pl.ds(pl.multiple_of(low * share, share), share)
                for group in range(groups):
                    lane = (group * count + chunk) * width
                    ordered[span, lane : lane + width] = parts[2 * chunk + i][group]

    columns = pl.ds(pl.multiple_of(pl.program_id(0) * block, block), block)
    out[...] = jnp.dot(
        ordered[...], factor[:, columns], preferred_element_type=F32
    ).astype(BF16)


def input_product(where, parts, factor, tokens):
    rank, depth = factor.shape
    block = min(depth, 512)
    values = [*parts, factor]
    return pl.pallas_call(
        functools.partial(input_kernel, len(parts) // 2),
        out_shape=jax.ShapeDtypeStruct((tokens, depth), BF16),
        grid=(depth // block,),
        in_specs=[pl.BlockSpec(memory_space=pltpu.SMEM)]
        + [pl.BlockSpec(memory_space=pltpu.VMEM)] * len(values),
        out_specs=pl.BlockSpec((tokens, block), lambda i: (0, i)),
        scratch_shapes=[pltpu.VMEM((tokens, rank), BF16)],
        compiler_params=pltpu.CompilerParams(vmem_limit_bytes=24 * MIB),
        cost_estimate=cost(2 * tokens * rank * depth, *values),
    )(where, *values)


def right_kernel(owners, near, scale, where, *refs):
    parts, refs = refs[:CHUNKS], refs[CHUNKS:]
    grads, refs = refs[: 2 * owners], refs[2 * owners :]
    done, (out, ordered) = refs[:-2], refs[-2:]
    share, width = parts[0].shape[1] // 2, parts[0].shape[2]
    block = out.shape[1]
    blocks = len(grads) * share

    @pl.when(pl.program_id(0) == 0)
    def _():
        for c, part in enumerate(parts):
            lanes = slice(c * width, (c + 1) * width)
            ordered[:, lanes] = part[...].reshape(blocks, width)

    low = where[0] if near else 1 - where[0]
    span = pl.ds(pl.multiple_of(low * share, share), share)
    columns = pl.ds(pl.multiple_of(pl.program_id(0) * block, block), block)
    total = None
    for i, grad in enumerate(grads):
        term = dot(ordered[i * share : (i + 1) * share, :], grad[span, columns], ROWS)
        total = term if total is None else total + term
    if done:
        total = (done[0][:, columns] + total) * scale
    out[...] = total


def right_rows(where, near, scale, parts, grads, done):
    owners, rows, width = parts[0].shape
    columns = grads[0].shape[1]
    block = min(columns, 512)
    values = [*parts, *grads, *done]
    return pl.pallas_call(
        functools.partial(right_kernel, owners, near, scale),
        out_shape=jax.ShapeDtypeStruct((CHUNKS * width, columns), F32),
        grid=(columns // block,),
        in_specs=[pl.BlockSpec(memory_space=pltpu.SMEM)]
        + [pl.BlockSpec(memory_space=pltpu.VMEM)] * len(values),
        out_specs=pl.BlockSpec((CHUNKS * width, block), lambda i: (0, i)),
        scratch_shapes=[pltpu.VMEM((owners * rows, CHUNKS * width), BF16)],
        compiler_params=pltpu.CompilerParams(vmem_limit_bytes=32 * MIB),
        cost_estimate=cost(2 * owners * rows * CHUNKS * width * columns, *parts, *grads),
    )(where, *values)


def final_kernel(scale, count, where, *refs):
    out = refs[-1]
    per = (len(refs) - 1) // count
    width = refs[0].shape[0]
    for chunk in range(count):
        total = refs[chunk * per][...]
        for other in refs[chunk * per + 1 : (chunk + 1) * per]:
            total = total + other[...].astype(F32)
        out[chunk * width : (chunk + 1) * width, :] = total * scale


def shards(activations, left_factor, right_factor, out_grad):
    groups = lax.axis_size("dp")
    width = lax.axis_size("tensor")
    tokens, depth = activations.shape
    rank = left_factor.shape[0]
    owners, peers = groups // 2, width // 2
    rows = rank // groups
    step = rows // CHUNKS
    scale = 1.0 / math.sqrt(tokens * groups)
    place, spot = lax.axis_index("tensor"), lax.axis_index("dp")
    where = jnp.stack([place % 2, place // 2, spot % 2, spot // 2, place // 2 % 2])
    where = where.astype(jnp.int32)
    run = InOrder()

    left_blocks = left_factor.reshape(owners, 2, CHUNKS, step, depth)
    right_blocks = right_factor.reshape(groups, CHUNKS, step, out_grad.shape[1])

    features = out_grad.shape[1]

    def grad_product(which, dtype, first, chunks, limit):
        return lambda *values: products(
            where,
            which,
            values,
            right_blocks,
            (groups, chunks, step, features),
            lambda i, where: (i, first, 0, 0),
            dtype,
            2,
            chunks,
            limit,
        )

    def latent_product(which, dtype):
        return lambda *values: products(
            where,
            which,
            values,
            left_blocks,
            (owners, 1, CHUNKS, step, depth),
            lambda i, where: (i, where[2], 0, 0, 0),
            dtype,
            owners,
            CHUNKS,
            24,
        )

    def halve(which, c):
        return 2 if HALVES[which][c] and peers > 1 else 1

    kept, piece, comes, near, far, latest = ({} for _ in range(6))
    theirs, left_mine, left_in = {}, {}, {}
    first_mask, masks = 2, []
    mask = 4
    while mask < width:
        masks.append(mask)
        mask *= 2

    def scoped(name, c, stage):
        return jax.named_scope(f"{NAMES[name]}{c}_{stage}")

    def grad_send(c, limit):
        with scoped("G", c, "S"):
            (away,) = run(grad_product(0, BF16, c, 1, limit), out_grad)
            comes["G", c] = latest["G", c] = swap(away, "tensor", 1)

    def grad_keep():
        with scoped("G", "", "K"):
            for c, value in enumerate(run(grad_product(1, F32, 0, CHUNKS, 24), out_grad)):
                kept["G", c] = value

    def latent_send():
        with scoped("L", "", "S"):
            for c, value in enumerate(run(latent_product(0, BF16), *acts)):
                comes["L", c] = latest["L", c] = swap(value, "tensor", 1)

    def latent_keep():
        with scoped("L", "", "K"):
            for c, value in enumerate(run(latent_product(1, F32), *acts)):
                kept["L", c] = value

    def near_sum(name, c):
        parts = halve(name, c)
        with scoped(name, c, "near"):
            piece[name, c], away = run(
                lambda a, b: split(where, parts, a, b), kept[name, c], comes[name, c]
            )
            comes[name, c] = latest[name, c] = swap(away, "tensor", first_mask)

    def far_sum(name, c):
        for mask in masks:
            with scoped(name, c, "far"):
                piece[name, c], away = run(
                    functools.partial(added, where), piece[name, c], comes[name, c]
                )
                comes[name, c] = latest[name, c] = swap(away, "tensor", mask)

    def last_sum(name, c):
        with scoped(name, c, "last"):
            if name == "G":
                piece[name, c] = run(
                    functools.partial(summed, where), piece[name, c], comes[name, c]
                )
                forward(name, c)
            else:
                own, *others = run(
                    functools.partial(summed_by_owner, where), piece[name, c], comes[name, c]
                )
                others = [swap(v, "dp", 2 * s) for s, v in enumerate(others, 1)]
                piece[name, c], latest[name, c] = [own, *others], others

    def forward(name, c):
        if halve(name, c) == 2:
            comes[name, c] = latest[name, c] = swap(piece[name, c], "tensor", first_mask)
        else:
            spread(name, c, piece[name, c])

    def spread(name, c, value):
        near[name, c] = value
        far[name, c] = latest[name, c] = swap(value, "tensor", 1)

    def stack(name, c):
        with scoped(name, c, "stack"):
            piece[name, c] = run(functools.partial(stacked, where), *piece[name, c])
            forward(name, c)

    def join(name, c):
        if halve(name, c) == 2:
            with scoped(name, c, "join"):
                spread(
                    name, c, run(functools.partial(joined, where), piece[name, c], comes[name, c])
                )

    def core_halves(c):
        with scoped("G", c, "halves"):
            theirs[c] = latest["G", c] = swap(
                run(lambda a, b: halves(where, owners, a, b), near["G", c], far["G", c]), "dp", 1
            )

    def left(c):
        with scoped("G", c, "left"):
            left_mine[c], out = run(
                lambda *v: left_parts(where, owners, *v),
                near["G", c],
                far["G", c],
                theirs[c],
                *acts,
            )
            left_in[c] = latest["G", c] = [swap(v, "dp", 2 * s) for s, v in enumerate(out, 1)]

    def inputs():
        with scoped("G", "", "input"):
            return run(
                lambda f, *v: input_product(where, v, f, tokens),
                left_factor,
                *(v for c in range(CHUNKS) for v in [near["G", c], far["G", c]]),
            )

    def rights(stage, *done):
        parts = near if stage == "rn" else far
        with scoped("L", "", stage):
            return run(
                lambda *v: right_rows(
                    where, stage == "rn", scale, v[:CHUNKS], v[CHUNKS : CHUNKS + 2 * owners], v[CHUNKS + 2 * owners :]
                ),
                *(parts["L", c] for c in range(CHUNKS)),
                *grads,
                *done,
            )

    def final():
        with scoped("G", "", "final"):
            return run(
                lambda *v: whole_call(
                    functools.partial(final_kernel, scale, CHUNKS), where, v, [((rows, depth), F32)]
                )[0],
                *(v for c in range(CHUNKS) for v in [left_mine[c], *left_in[c]]),
            )

    def settle(*values):
        run.last = (run.last, values)

    with scoped("x", "", "og"):
        far_grads = [swap(out_grad, "dp", 2 * s) for s in range(1, owners)]
    with scoped("c", "", "acts"):
        acts = (activations, swap(activations, "dp", 1))
    with scoped("c", "", "own"):
        grads = [out_grad, swap(out_grad, "dp", 1)]

    def far_swaps():
        with scoped("c", "", "far"):
            for block in far_grads:
                grads.extend([block, swap(tied(block, run), "dp", 1)])
    input_grad = right_grad = left_grad = None
    actions = {
        "near": near_sum,
        "far": far_sum,
        "last": last_sum,
        "join": join,
        "stack": stack,
    }
    for entry in ORDER:
        if entry == "GK":
            grad_keep()
        elif entry == "LS":
            latent_send()
        elif entry == "LK":
            latent_keep()
        elif entry == "Lrn":
            right_near = rights("rn")
        elif entry == "Lrf":
            right_grad = rights("rf", right_near)
        elif entry == "input":
            input_grad = inputs()
        elif entry == "final":
            left_grad = final()
        elif entry == "own":
            settle(grads[1])
        elif entry == "og":
            far_swaps()
        elif entry == "@og":
            settle(*grads)
        elif entry[0] == "@":
            settle(latest[entry[1], int(entry[2])])
        else:
            name, c, stage = entry[0], int(entry[1]), entry[2:]
            if stage == "S":
                grad_send(c, 24)
            elif stage == "halves":
                core_halves(c)
            elif stage == "left":
                left(c)
            else:
                actions[stage](name, c)
    return input_grad, left_grad, right_grad


def solution(mesh):
    placed = (P("dp", "tensor"), P(None, "tensor"), P(None, "tensor"), P("dp", "tensor"))
    return jax.shard_map(
        shards,
        mesh=mesh,
        in_specs=placed,
        out_specs=(P("dp", "tensor"), P("dp", "tensor"), P("dp", "tensor")),
        check_vma=False,
    )
```

```python
import functools
import math

import jax
import jax.numpy as jnp
from jax import lax
from jax.experimental import pallas as pl
from jax.experimental.pallas import tpu as pltpu
from jax.sharding import PartitionSpec as P

CHUNKS = 2
NAMES = {"G": "latent_grad", "L": "latent", "x": "far", "c": "core"}
PIECES = 4
ORDER = (
    "own", "acts", "far", "G1S", "G0S", "GK", "LS", "@own", "LK", "G0near", "G1near", "G0far",
    "L0near", "G1far", "L1near", "L0far", "G0last", "@G1", "G1last", "L1far", "G0join",
    "L0last", "G1join", "L0stack", "L1last", "G0halves", "L0join", "og", "L1stack", "G1halves",
    "G0left", "L1join", "G1left", "input", "Lrn", "Lrf", "final",
)
HALVES = {"G": (True, True), "L": (True, True)}
BF16 = jnp.bfloat16
F32 = jnp.float32
MIB = 1 << 20
COLS = (((1,), (1,)), ((), ()))
ROWS = (((0,), (0,)), ((), ()))


def dot(first, second, dims):
    return lax.dot_general(first, second, dims, preferred_element_type=F32)


def cost(flops, *arrays):
    sizes = []
    for array in arrays:
        shape, dtype = array if isinstance(array, tuple) else (array.shape, array.dtype)
        sizes.append(math.prod(shape) * jnp.dtype(dtype).itemsize)
    return pl.CostEstimate(flops=flops, bytes_accessed=sum(sizes), transcendentals=0)


def whole_call(kernel, where, values, outs, scratch=(), flops=0):
    return pl.pallas_call(
        kernel,
        out_shape=[jax.ShapeDtypeStruct(s, t) for s, t in outs],
        in_specs=[pl.BlockSpec(memory_space=pltpu.SMEM)]
        + [pl.BlockSpec(memory_space=pltpu.VMEM)] * len(values),
        out_specs=[pl.BlockSpec(memory_space=pltpu.VMEM)] * len(outs),
        scratch_shapes=list(scratch),
        compiler_params=pltpu.CompilerParams(vmem_limit_bytes=24 * MIB),
        cost_estimate=cost(flops, *values, *outs),
    )(where, *values)


def swap(value, axis, mask):
    size = lax.axis_size(axis)
    return lax.ppermute(value, axis, [(i, i ^ mask) for i in range(size)])


def tied(value, run):
    return lax.optimization_barrier((value, run.last))[0]


class InOrder:
    def __init__(self):
        self.last = ()

    def __call__(self, step, *values):
        values, _ = lax.optimization_barrier((values, self.last))
        result = step(*values)
        self.last = result
        return result


def product_kernel(chunks, where, *refs):
    values, factor, outs = refs[:-chunks - 1], refs[-chunks - 1], refs[-chunks:]
    count, width = outs[0].shape[0], outs[0].shape[2]
    flat = factor[...].reshape(count * chunks * width, factor.shape[-1])
    rows = values[0].shape[0]
    for i, value in enumerate(values):
        result = dot(value[...], flat, COLS)
        for j in range(count):
            for c in range(chunks):
                lane = (j * chunks + c) * width
                part = result[:, lane : lane + width]
                outs[c][j, i * rows : (i + 1) * rows, :] = part.astype(outs[c].dtype)


def products(where, which, values, factor, block, place, dtype, batch, chunks, limit):
    rows, depth = values[0].shape
    half = rows // 2
    width = block[-2]
    count = math.prod(block[:-3])
    total = half * len(values)

    def half_of(i, where):
        return (where[0] if which else 1 - where[0], 0)

    return pl.pallas_call(
        functools.partial(product_kernel, chunks),
        out_shape=[jax.ShapeDtypeStruct((count, total, width), dtype)] * chunks,
        grid_spec=pltpu.PrefetchScalarGridSpec(
            num_scalar_prefetch=1,
            grid=(count // batch,),
            in_specs=[pl.BlockSpec((half, depth), half_of)] * len(values)
            + [pl.BlockSpec((batch,) + block[1:], place)],
            out_specs=[pl.BlockSpec((batch, total, width), lambda i, where: (i, 0, 0))] * chunks,
        ),
        compiler_params=pltpu.CompilerParams(vmem_limit_bytes=limit * MIB),
        cost_estimate=cost(
            2 * total * depth * count * chunks * width,
            *values,
            ((count, chunks, width, depth), BF16),
        ),
    )(where, *values, factor)


def split_kernel(where, kept, sent, mine, away):
    rows = mine.shape[1]
    if rows == kept.shape[1]:
        total = kept[...] + sent[...].astype(F32)
        mine[...] = total
        away[...] = total.astype(BF16)
        return
    for out, at in ((mine, where[4]), (away, 1 - where[4])):
        span = pl.ds(pl.multiple_of(at * rows, rows), rows)
        out[...] = (kept[:, span, :] + sent[:, span, :].astype(F32)).astype(out.dtype)


def split(where, parts, kept, sent):
    count, rows, width = kept.shape
    shape = (count, rows // parts, width)
    return whole_call(split_kernel, where, [kept, sent], [(shape, F32), (shape, BF16)])


def added_kernel(where, mine, other, out, away):
    total = mine[...] + other[...].astype(F32)
    out[...] = total
    away[...] = total.astype(BF16)


def added(where, mine, other):
    return whole_call(
        added_kernel, where, [mine, other], [(mine.shape, F32), (mine.shape, BF16)]
    )


def summed_kernel(where, mine, other, out):
    out[...] = (mine[...] + other[...].astype(F32)).astype(BF16)


def summed(where, mine, other):
    return whole_call(summed_kernel, where, [mine, other], [(mine.shape, BF16)])[0]


def summed_by_owner_kernel(where, mine, other, *outs):
    for step, out in enumerate(outs):
        at = where[3] ^ step
        out[...] = (mine[at] + other[at].astype(F32)).astype(BF16)


def summed_by_owner(where, mine, other):
    owners = mine.shape[0]
    return whole_call(
        summed_by_owner_kernel, where, [mine, other], [(mine.shape[1:], BF16)] * owners
    )


def stacked_kernel(where, *refs):
    *pieces, out = refs
    for i, piece in enumerate(pieces):
        out[i] = piece[...]


def stacked(where, *pieces):
    return whole_call(
        stacked_kernel, where, list(pieces), [((len(pieces),) + pieces[0].shape, BF16)]
    )[0]


def joined_kernel(where, mine, other, out):
    rows = mine.shape[1]
    for part, at in ((mine, where[4]), (other, 1 - where[4])):
        out[:, pl.ds(pl.multiple_of(at * rows, rows), rows), :] = part[...]


def joined(where, mine, other):
    count, rows, width = mine.shape
    return whole_call(joined_kernel, where, [mine, other], [((count, 2 * rows, width), BF16)])[0]


def halves_kernel(owners, where, near, far, out):
    for i, part in enumerate((near, far)):
        for owner in range(owners):
            out[i, owner] = part[owner * 2 + 1 - where[2]]


def halves(where, owners, near, far):
    return whole_call(
        functools.partial(halves_kernel, owners),
        where,
        [near, far],
        [((2, owners) + near.shape[1:], BF16)],
    )[0]


def left_kernel(owners, where, near, far, theirs, acts, acts_other, mine, *rest):
    blocks, (ordered, result) = rest[: owners - 1], rest[owners - 1 :]
    _, share, width = near.shape
    for i, part in enumerate((near, far)):
        low = where[0] if i == 0 else 1 - where[0]
        span = pl.ds(pl.multiple_of(low * share, share), share)
        for owner in range(owners):
            lanes = slice(owner * width, (owner + 1) * width)
            ordered[0, span, lanes] = part[owner * 2 + where[2]]
            ordered[1, span, lanes] = theirs[i, owner]
    result[...] = dot(ordered[0], acts[...], ROWS) + dot(ordered[1], acts_other[...], ROWS)
    for step in range(owners):
        rows = pl.ds(pl.multiple_of((where[3] ^ step) * width, width), width)
        if step:
            blocks[step - 1][...] = result[rows, :].astype(BF16)
        else:
            mine[...] = result[rows, :]


def left_parts(where, owners, near, far, theirs, acts, acts_other):
    width = near.shape[-1]
    tokens, depth = acts.shape
    mine, *blocks = whole_call(
        functools.partial(left_kernel, owners),
        where,
        [near, far, theirs, acts, acts_other],
        [((width, depth), F32)] + [((width, depth), BF16)] * (owners - 1),
        [
            pltpu.VMEM((2, tokens, owners * width), BF16),
            pltpu.VMEM((owners * width, depth), F32),
        ],
        4 * tokens * owners * width * depth,
    )
    return mine, blocks


def written_call(kernel, where, values, out, blocks, scratch, flops, limit):
    shape, dtype = out
    return pl.pallas_call(
        kernel,
        out_shape=jax.ShapeDtypeStruct(shape, dtype),
        in_specs=[pl.BlockSpec(memory_space=pltpu.SMEM)]
        + [pl.BlockSpec(memory_space=pltpu.VMEM)] * len(values),
        out_specs=pl.BlockSpec(memory_space=pltpu.HBM),
        scratch_shapes=[
            pltpu.VMEM(shape, dtype),
            pltpu.SemaphoreType.DMA((blocks,)),
            *scratch,
        ],
        compiler_params=pltpu.CompilerParams(vmem_limit_bytes=limit * MIB),
        cost_estimate=cost(flops, *values),
    )(where, *values)


def write(held, out, sems, i, index):
    copy = pltpu.make_async_copy(held.at[index], out.at[index], sems.at[i])
    copy.start()
    return copy


def input_kernel(count, blocks, where, *refs):
    parts, (factor, out, held, sems, ordered) = refs[: 2 * count], refs[2 * count :]
    groups, share, width = parts[0].shape
    block = held.shape[1] // blocks
    for chunk in range(count):
        for i in range(2):
            low = where[0] if i == 0 else 1 - where[0]
            span = pl.ds(pl.multiple_of(low * share, share), share)
            for group in range(groups):
                lane = (group * count + chunk) * width
                ordered[span, lane : lane + width] = parts[2 * chunk + i][group]
    copies = []
    for i in range(blocks):
        columns = slice(i * block, (i + 1) * block)
        held[:, columns] = jnp.dot(
            ordered[...], factor[:, columns], preferred_element_type=F32
        ).astype(BF16)
        copies.append(write(held, out, sems, i, (slice(None), columns)))
    for copy in copies:
        copy.wait()


def input_product(where, parts, factor, tokens):
    rank, depth = factor.shape
    blocks = max(depth // 256, 1)
    return written_call(
        functools.partial(input_kernel, len(parts) // 2, blocks),
        where,
        [*parts, factor],
        ((tokens, depth), BF16),
        blocks,
        [pltpu.VMEM((tokens, rank), BF16)],
        2 * tokens * rank * depth,
        16,
    )


def right_sum(low, parts, grads, ordered, columns):
    share = parts[0].shape[1] // 2
    span = pl.ds(pl.multiple_of(low * share, share), share)
    total = None
    refs = list(grads)
    for i in range(ordered.shape[0] // share):
        pieces = [refs.pop(0) for _ in range(pieces_of(i))]
        width = pieces[0].shape[1]
        at, start = divmod(columns.start, width)
        grad = pieces[at][span, start : start + columns.stop - columns.start]
        term = dot(ordered[i * share : (i + 1) * share, :], grad, ROWS)
        total = term if total is None else total + term
    return total


def pieces_of(i):
    return PIECES if i >= 2 and i % 2 else 1


def order_parts(parts, ordered):
    width = parts[0].shape[2]
    for c, part in enumerate(parts):
        ordered[:, c * width : (c + 1) * width] = part[...].reshape(ordered.shape[0], width)


def right_near_kernel(blocks, where, *refs):
    parts, grads, (out, ordered) = refs[:CHUNKS], refs[CHUNKS:-2], refs[-2:]
    block = out.shape[1] // blocks
    order_parts(parts, ordered)
    for i in range(blocks):
        columns = slice(i * block, (i + 1) * block)
        out[:, columns] = right_sum(where[0], parts, grads, ordered, columns)


def right_near(where, parts, grads):
    owners, rows, width = parts[0].shape
    columns = grads[0].shape[1]
    return whole_call(
        functools.partial(right_near_kernel, max(columns // 512, PIECES)),
        where,
        [*parts, *grads],
        [((CHUNKS * width, columns), F32)],
        [pltpu.VMEM((owners * rows, CHUNKS * width), BF16)],
        2 * owners * rows * CHUNKS * width * columns,
    )[0]


def right_far_kernel(blocks, scale, where, *refs):
    parts, refs = refs[:CHUNKS], refs[CHUNKS:]
    grads, (done, out, held, sems, ordered) = refs[:-5], refs[-5:]
    block = held.shape[1] // blocks
    order_parts(parts, ordered)
    copies = []
    for i in range(blocks):
        columns = slice(i * block, (i + 1) * block)
        total = done[:, columns] + right_sum(1 - where[0], parts, grads, ordered, columns)
        held[:, columns] = total * scale
        copies.append(write(held, out, sems, i, (slice(None), columns)))
    for copy in copies:
        copy.wait()


def right_far(where, scale, parts, grads, done):
    owners, rows, width = parts[0].shape
    columns = grads[0].shape[1]
    blocks = max(columns // 256, PIECES)
    return written_call(
        functools.partial(right_far_kernel, blocks, scale),
        where,
        [*parts, *grads, done],
        (done.shape, F32),
        blocks,
        [pltpu.VMEM((owners * rows, CHUNKS * width), BF16)],
        2 * owners * rows * CHUNKS * width * columns,
        24,
    )


def final_kernel(scale, count, where, *refs):
    refs, (out, held, sems) = refs[:-3], refs[-3:]
    per = len(refs) // count
    width = refs[0].shape[0]
    copies = []
    for chunk in range(count):
        total = refs[chunk * per][...]
        for other in refs[chunk * per + 1 : (chunk + 1) * per]:
            total = total + other[...].astype(F32)
        rows = slice(chunk * width, (chunk + 1) * width)
        held[rows, :] = total * scale
        copies.append(write(held, out, sems, chunk, (rows, slice(None))))
    for copy in copies:
        copy.wait()


def left_final(where, scale, values, shape):
    return written_call(
        functools.partial(final_kernel, scale, CHUNKS), where, values, (shape, F32), CHUNKS, [], 0, 16
    )


def shards(activations, left_factor, right_factor, out_grad):
    groups = lax.axis_size("dp")
    width = lax.axis_size("tensor")
    tokens, depth = activations.shape
    rank = left_factor.shape[0]
    owners, peers = groups // 2, width // 2
    rows = rank // groups
    step = rows // CHUNKS
    scale = 1.0 / math.sqrt(tokens * groups)
    place, spot = lax.axis_index("tensor"), lax.axis_index("dp")
    where = jnp.stack([place % 2, place // 2, spot % 2, spot // 2, place // 2 % 2])
    where = where.astype(jnp.int32)
    run = InOrder()

    left_blocks = left_factor.reshape(owners, 2, CHUNKS, step, depth)
    right_blocks = right_factor.reshape(groups, CHUNKS, step, out_grad.shape[1])

    features = out_grad.shape[1]

    def grad_product(which, dtype, first, chunks, limit):
        return lambda *values: products(
            where,
            which,
            values,
            right_blocks,
            (groups, chunks, step, features),
            lambda i, where: (i, first, 0, 0),
            dtype,
            2,
            chunks,
            limit,
        )

    def latent_product(which, dtype):
        return lambda *values: products(
            where,
            which,
            values,
            left_blocks,
            (owners, 1, CHUNKS, step, depth),
            lambda i, where: (i, where[2], 0, 0, 0),
            dtype,
            owners,
            CHUNKS,
            24,
        )

    def halve(which, c):
        return 2 if HALVES[which][c] and peers > 1 else 1

    kept, piece, comes, near, far, latest = ({} for _ in range(6))
    theirs, left_mine, left_in = {}, {}, {}
    first_mask, masks = 2, []
    mask = 4
    while mask < width:
        masks.append(mask)
        mask *= 2

    def scoped(name, c, stage):
        return jax.named_scope(f"{NAMES[name]}{c}_{stage}")

    def grad_send(c):
        with scoped("G", c, "S"):
            (away,) = run(grad_product(0, BF16, c, 1, 24), out_grad)
            comes["G", c] = latest["G", c] = swap(away, "tensor", 1)

    def grad_keep():
        with scoped("G", "", "K"):
            for c, value in enumerate(run(grad_product(1, F32, 0, CHUNKS, 24), out_grad)):
                kept["G", c] = value

    def latent_send():
        with scoped("L", "", "S"):
            for c, value in enumerate(run(latent_product(0, BF16), *acts)):
                comes["L", c] = latest["L", c] = swap(value, "tensor", 1)

    def latent_keep():
        with scoped("L", "", "K"):
            for c, value in enumerate(run(latent_product(1, F32), *acts)):
                kept["L", c] = value

    def near_sum(name, c):
        parts = halve(name, c)
        with scoped(name, c, "near"):
            piece[name, c], away = run(
                lambda a, b: split(where, parts, a, b), kept[name, c], comes[name, c]
            )
            comes[name, c] = latest[name, c] = swap(away, "tensor", first_mask)

    def far_sum(name, c):
        for mask in masks:
            with scoped(name, c, "far"):
                piece[name, c], away = run(
                    functools.partial(added, where), piece[name, c], comes[name, c]
                )
                comes[name, c] = latest[name, c] = swap(away, "tensor", mask)

    def last_sum(name, c):
        with scoped(name, c, "last"):
            if name == "G":
                piece[name, c] = run(
                    functools.partial(summed, where), piece[name, c], comes[name, c]
                )
                forward(name, c)
            else:
                own, *others = run(
                    functools.partial(summed_by_owner, where), piece[name, c], comes[name, c]
                )
                others = [swap(v, "dp", 2 * s) for s, v in enumerate(others, 1)]
                piece[name, c], latest[name, c] = [own, *others], others

    def forward(name, c):
        if halve(name, c) == 2:
            comes[name, c] = latest[name, c] = swap(piece[name, c], "tensor", first_mask)
        else:
            spread(name, c, piece[name, c])

    def spread(name, c, value):
        near[name, c] = value
        far[name, c] = latest[name, c] = swap(value, "tensor", 1)

    def stack(name, c):
        with scoped(name, c, "stack"):
            piece[name, c] = run(functools.partial(stacked, where), *piece[name, c])
            forward(name, c)

    def join(name, c):
        if halve(name, c) == 2:
            with scoped(name, c, "join"):
                spread(
                    name, c, run(functools.partial(joined, where), piece[name, c], comes[name, c])
                )

    def core_halves(c):
        with scoped("G", c, "halves"):
            theirs[c] = latest["G", c] = swap(
                run(lambda a, b: halves(where, owners, a, b), near["G", c], far["G", c]), "dp", 1
            )

    def left(c):
        with scoped("G", c, "left"):
            left_mine[c], out = run(
                lambda *v: left_parts(where, owners, *v),
                near["G", c],
                far["G", c],
                theirs[c],
                *acts,
            )
            left_in[c] = latest["G", c] = [swap(v, "dp", 2 * s) for s, v in enumerate(out, 1)]

    def inputs():
        with scoped("G", "", "input"):
            return run(
                lambda f, *v: input_product(where, v, f, tokens),
                left_factor,
                *(v for c in range(CHUNKS) for v in [near["G", c], far["G", c]]),
            )

    def rights_near():
        with scoped("L", "", "rn"):
            return run(
                lambda *v: right_near(where, v[:CHUNKS], v[CHUNKS:]),
                *(near["L", c] for c in range(CHUNKS)),
                *grads,
            )

    def rights_far(done):
        with scoped("L", "", "rf"):
            return run(
                lambda d, *v: right_far(where, scale, v[:CHUNKS], v[CHUNKS:], d),
                done,
                *(far["L", c] for c in range(CHUNKS)),
                *grads,
            )

    def final():
        with scoped("G", "", "final"):
            return run(
                lambda *v: left_final(where, scale, v, (rows, depth)),
                *(v for c in range(CHUNKS) for v in [left_mine[c], *left_in[c]]),
            )

    def settle(*values):
        run.last = (run.last, values)

    far_grads, acts, grads = [], [activations], [out_grad]

    def far_start():
        with scoped("x", "", "og"):
            for s in range(1, owners):
                far_grads.append(swap(tied(out_grad, run), "dp", 2 * s))

    def acts_swap():
        with scoped("c", "", "acts"):
            acts.append(swap(tied(activations, run), "dp", 1))

    def own_swap():
        with scoped("c", "", "own"):
            grads.append(swap(tied(out_grad, run), "dp", 1))

    def far_swaps():
        with scoped("c", "", "far"):
            for block in far_grads:
                width = block.shape[1] // PIECES
                grads.append(block)
                for i in range(PIECES):
                    grads.append(swap(block[:, i * width : (i + 1) * width], "dp", 1))
    input_grad = right_grad = left_grad = None
    actions = {
        "near": near_sum,
        "far": far_sum,
        "last": last_sum,
        "join": join,
        "stack": stack,
    }
    for entry in ORDER:
        if entry == "GK":
            grad_keep()
        elif entry == "LS":
            latent_send()
        elif entry == "LK":
            latent_keep()
        elif entry == "Lrn":
            right_near_sum = rights_near()
        elif entry == "Lrf":
            right_grad = rights_far(right_near_sum)
        elif entry == "input":
            input_grad = inputs()
        elif entry == "final":
            left_grad = final()
        elif entry == "own":
            own_swap()
        elif entry == "acts":
            acts_swap()
        elif entry == "far":
            far_start()
        elif entry == "@own":
            settle(grads[1])
        elif entry == "og":
            far_swaps()
        elif entry == "@og":
            settle(*grads)
        elif entry[0] == "@":
            settle(latest[entry[1], int(entry[2])])
        else:
            name, c, stage = entry[0], int(entry[1]), entry[2:]
            if stage == "S":
                grad_send(c)
            elif stage == "halves":
                core_halves(c)
            elif stage == "left":
                left(c)
            else:
                actions[stage](name, c)
    return input_grad, left_grad, right_grad


def solution(mesh):
    placed = (P("dp", "tensor"), P(None, "tensor"), P(None, "tensor"), P("dp", "tensor"))
    return jax.shard_map(
        shards,
        mesh=mesh,
        in_specs=placed,
        out_specs=(P("dp", "tensor"), P("dp", "tensor"), P("dp", "tensor")),
        check_vma=False,
    )
```

```python
import functools
import math

import jax
import jax.numpy as jnp
from jax import lax
from jax.experimental import pallas as pl
from jax.experimental.pallas import tpu as pltpu
from jax.sharding import PartitionSpec as P

CHUNKS = 2
NAMES = {"G": "latent_grad", "L": "latent", "x": "far", "c": "core"}
PIECES = 4
ORDER = (
    "own", "acts", "far", "G0S", "G1S", "GK", "LS", "@own", "LK", "G0near", "G1near", "G0far",
    "L0near", "G1far", "L1near", "G0last", "L0far", "G1last", "L1far", "G0join", "L0last",
    "G1join", "L0stack", "L1last", "G0halves", "L0join", "og", "L1stack", "G1halves", "G0left",
    "L1join", "G1left", "input", "Lrn", "Lrf", "final",
)
HALVES = {"G": (True, True), "L": (True, True)}
BF16 = jnp.bfloat16
F32 = jnp.float32
MIB = 1 << 20
COLS = (((1,), (1,)), ((), ()))
ROWS = (((0,), (0,)), ((), ()))


def dot(first, second, dims):
    return lax.dot_general(first, second, dims, preferred_element_type=F32)


def cost(flops, *arrays):
    sizes = []
    for array in arrays:
        shape, dtype = array if isinstance(array, tuple) else (array.shape, array.dtype)
        sizes.append(math.prod(shape) * jnp.dtype(dtype).itemsize)
    return pl.CostEstimate(flops=flops, bytes_accessed=sum(sizes), transcendentals=0)


def whole_call(kernel, where, values, outs, scratch=(), flops=0):
    return pl.pallas_call(
        kernel,
        out_shape=[jax.ShapeDtypeStruct(s, t) for s, t in outs],
        in_specs=[pl.BlockSpec(memory_space=pltpu.SMEM)]
        + [pl.BlockSpec(memory_space=pltpu.VMEM)] * len(values),
        out_specs=[pl.BlockSpec(memory_space=pltpu.VMEM)] * len(outs),
        scratch_shapes=list(scratch),
        compiler_params=pltpu.CompilerParams(vmem_limit_bytes=24 * MIB),
        cost_estimate=cost(flops, *values, *outs),
    )(where, *values)


def swap(value, axis, mask):
    size = lax.axis_size(axis)
    return lax.ppermute(value, axis, [(i, i ^ mask) for i in range(size)])


def tied(value, run):
    return lax.optimization_barrier((value, run.last))[0]


class InOrder:
    def __init__(self):
        self.last = ()
        self.free = False

    def __call__(self, step, *values):
        if self.free:
            return step(*values)
        values, _ = lax.optimization_barrier((values, self.last))
        result = step(*values)
        self.last = result
        return result


def product_kernel(chunks, where, *refs):
    values, factor, outs = refs[:-chunks - 1], refs[-chunks - 1], refs[-chunks:]
    count, width = outs[0].shape[0], outs[0].shape[2]
    flat = factor[...].reshape(count * chunks * width, factor.shape[-1])
    rows = values[0].shape[0]
    for i, value in enumerate(values):
        result = dot(value[...], flat, COLS)
        for j in range(count):
            for c in range(chunks):
                lane = (j * chunks + c) * width
                part = result[:, lane : lane + width]
                outs[c][j, i * rows : (i + 1) * rows, :] = part.astype(outs[c].dtype)


def products(where, which, values, factor, block, place, dtype, batch, chunks, limit):
    rows, depth = values[0].shape
    half = rows // 2
    width = block[-2]
    count = math.prod(block[:-3])
    total = half * len(values)

    def half_of(i, where):
        return (where[0] if which else 1 - where[0], 0)

    return pl.pallas_call(
        functools.partial(product_kernel, chunks),
        out_shape=[jax.ShapeDtypeStruct((count, total, width), dtype)] * chunks,
        grid_spec=pltpu.PrefetchScalarGridSpec(
            num_scalar_prefetch=1,
            grid=(count // batch,),
            in_specs=[pl.BlockSpec((half, depth), half_of)] * len(values)
            + [pl.BlockSpec((batch,) + block[1:], place)],
            out_specs=[pl.BlockSpec((batch, total, width), lambda i, where: (i, 0, 0))] * chunks,
        ),
        compiler_params=pltpu.CompilerParams(vmem_limit_bytes=limit * MIB),
        cost_estimate=cost(
            2 * total * depth * count * chunks * width,
            *values,
            ((count, chunks, width, depth), BF16),
        ),
    )(where, *values, factor)


def split_kernel(where, kept, sent, mine, away):
    rows = mine.shape[1]
    if rows == kept.shape[1]:
        total = kept[...] + sent[...].astype(F32)
        mine[...] = total
        away[...] = total.astype(BF16)
        return
    for out, at in ((mine, where[4]), (away, 1 - where[4])):
        span = pl.ds(pl.multiple_of(at * rows, rows), rows)
        out[...] = (kept[:, span, :] + sent[:, span, :].astype(F32)).astype(out.dtype)


def split(where, parts, kept, sent):
    count, rows, width = kept.shape
    shape = (count, rows // parts, width)
    return whole_call(split_kernel, where, [kept, sent], [(shape, F32), (shape, BF16)])


def added_kernel(where, mine, other, out, away):
    total = mine[...] + other[...].astype(F32)
    out[...] = total
    away[...] = total.astype(BF16)


def added(where, mine, other):
    return whole_call(
        added_kernel, where, [mine, other], [(mine.shape, F32), (mine.shape, BF16)]
    )


def summed_kernel(where, mine, other, out):
    out[...] = (mine[...] + other[...].astype(F32)).astype(BF16)


def summed(where, mine, other):
    return whole_call(summed_kernel, where, [mine, other], [(mine.shape, BF16)])[0]


def summed_by_owner_kernel(where, mine, other, *outs):
    for step, out in enumerate(outs):
        at = where[3] ^ step
        out[...] = (mine[at] + other[at].astype(F32)).astype(BF16)


def summed_by_owner(where, mine, other):
    owners = mine.shape[0]
    return whole_call(
        summed_by_owner_kernel, where, [mine, other], [(mine.shape[1:], BF16)] * owners
    )


def stacked_kernel(where, *refs):
    *pieces, out = refs
    for i, piece in enumerate(pieces):
        out[i] = piece[...]


def stacked(where, *pieces):
    return whole_call(
        stacked_kernel, where, list(pieces), [((len(pieces),) + pieces[0].shape, BF16)]
    )[0]


def joined_kernel(where, mine, other, out):
    rows = mine.shape[1]
    for part, at in ((mine, where[4]), (other, 1 - where[4])):
        out[:, pl.ds(pl.multiple_of(at * rows, rows), rows), :] = part[...]


def joined(where, mine, other):
    count, rows, width = mine.shape
    return whole_call(joined_kernel, where, [mine, other], [((count, 2 * rows, width), BF16)])[0]


def halves_kernel(owners, where, near, far, out):
    for i, part in enumerate((near, far)):
        for owner in range(owners):
            out[i, owner] = part[owner * 2 + 1 - where[2]]


def halves(where, owners, near, far):
    return whole_call(
        functools.partial(halves_kernel, owners),
        where,
        [near, far],
        [((2, owners) + near.shape[1:], BF16)],
    )[0]


def left_kernel(owners, where, near, far, theirs, acts, acts_other, mine, *rest):
    blocks, (ordered, result) = rest[: owners - 1], rest[owners - 1 :]
    _, share, width = near.shape
    for i, part in enumerate((near, far)):
        low = where[0] if i == 0 else 1 - where[0]
        span = pl.ds(pl.multiple_of(low * share, share), share)
        for owner in range(owners):
            lanes = slice(owner * width, (owner + 1) * width)
            ordered[0, span, lanes] = part[owner * 2 + where[2]]
            ordered[1, span, lanes] = theirs[i, owner]
    result[...] = dot(ordered[0], acts[...], ROWS) + dot(ordered[1], acts_other[...], ROWS)
    for step in range(owners):
        rows = pl.ds(pl.multiple_of((where[3] ^ step) * width, width), width)
        if step:
            blocks[step - 1][...] = result[rows, :].astype(BF16)
        else:
            mine[...] = result[rows, :]


def left_parts(where, owners, near, far, theirs, acts, acts_other):
    width = near.shape[-1]
    tokens, depth = acts.shape
    mine, *blocks = whole_call(
        functools.partial(left_kernel, owners),
        where,
        [near, far, theirs, acts, acts_other],
        [((width, depth), F32)] + [((width, depth), BF16)] * (owners - 1),
        [
            pltpu.VMEM((2, tokens, owners * width), BF16),
            pltpu.VMEM((owners * width, depth), F32),
        ],
        4 * tokens * owners * width * depth,
    )
    return mine, blocks


def written_call(kernel, where, values, out, blocks, scratch, flops, limit):
    shape, dtype = out
    return pl.pallas_call(
        kernel,
        out_shape=jax.ShapeDtypeStruct(shape, dtype),
        in_specs=[pl.BlockSpec(memory_space=pltpu.SMEM)]
        + [pl.BlockSpec(memory_space=pltpu.VMEM)] * len(values),
        out_specs=pl.BlockSpec(memory_space=pltpu.HBM),
        scratch_shapes=[
            pltpu.VMEM(shape, dtype),
            pltpu.SemaphoreType.DMA((blocks,)),
            *scratch,
        ],
        compiler_params=pltpu.CompilerParams(vmem_limit_bytes=limit * MIB),
        cost_estimate=cost(flops, *values),
    )(where, *values)


def write(held, out, sems, i, index):
    copy = pltpu.make_async_copy(held.at[index], out.at[index], sems.at[i])
    copy.start()
    return copy


def input_kernel(count, blocks, where, *refs):
    parts, (factor, out, held, sems, ordered) = refs[: 2 * count], refs[2 * count :]
    groups, share, width = parts[0].shape
    block = held.shape[1] // blocks
    for chunk in range(count):
        for i in range(2):
            low = where[0] if i == 0 else 1 - where[0]
            span = pl.ds(pl.multiple_of(low * share, share), share)
            for group in range(groups):
                lane = (group * count + chunk) * width
                ordered[span, lane : lane + width] = parts[2 * chunk + i][group]
    copies = []
    for i in range(blocks):
        columns = slice(i * block, (i + 1) * block)
        held[:, columns] = jnp.dot(
            ordered[...], factor[:, columns], preferred_element_type=F32
        ).astype(BF16)
        copies.append(write(held, out, sems, i, (slice(None), columns)))
    for copy in copies:
        copy.wait()


def input_product(where, parts, factor, tokens):
    rank, depth = factor.shape
    blocks = max(depth // 256, 1)
    return written_call(
        functools.partial(input_kernel, len(parts) // 2, blocks),
        where,
        [*parts, factor],
        ((tokens, depth), BF16),
        blocks,
        [pltpu.VMEM((tokens, rank), BF16)],
        2 * tokens * rank * depth,
        16,
    )


def right_sum(low, parts, grads, ordered, columns):
    share = parts[0].shape[1] // 2
    span = pl.ds(pl.multiple_of(low * share, share), share)
    total = None
    refs = list(grads)
    for i in range(ordered.shape[0] // share):
        pieces = [refs.pop(0) for _ in range(pieces_of(i))]
        width = pieces[0].shape[1]
        at, start = divmod(columns.start, width)
        grad = pieces[at][span, start : start + columns.stop - columns.start]
        term = dot(ordered[i * share : (i + 1) * share, :], grad, ROWS)
        total = term if total is None else total + term
    return total


def pieces_of(i):
    return PIECES if i >= 2 and i % 2 else 1


def order_parts(parts, ordered):
    width = parts[0].shape[2]
    for c, part in enumerate(parts):
        ordered[:, c * width : (c + 1) * width] = part[...].reshape(ordered.shape[0], width)


def right_near_kernel(blocks, where, *refs):
    parts, grads, (out, ordered) = refs[:CHUNKS], refs[CHUNKS:-2], refs[-2:]
    block = out.shape[1] // blocks
    order_parts(parts, ordered)
    for i in range(blocks):
        columns = slice(i * block, (i + 1) * block)
        out[:, columns] = right_sum(where[0], parts, grads, ordered, columns)


def right_near(where, parts, grads):
    owners, rows, width = parts[0].shape
    columns = grads[0].shape[1]
    return whole_call(
        functools.partial(right_near_kernel, max(columns // 512, PIECES)),
        where,
        [*parts, *grads],
        [((CHUNKS * width, columns), F32)],
        [pltpu.VMEM((owners * rows, CHUNKS * width), BF16)],
        2 * owners * rows * CHUNKS * width * columns,
    )[0]


def right_far_kernel(blocks, scale, where, *refs):
    parts, refs = refs[:CHUNKS], refs[CHUNKS:]
    grads, (done, out, held, sems, ordered) = refs[:-5], refs[-5:]
    block = held.shape[1] // blocks
    order_parts(parts, ordered)
    copies = []
    for i in range(blocks):
        columns = slice(i * block, (i + 1) * block)
        total = done[:, columns] + right_sum(1 - where[0], parts, grads, ordered, columns)
        held[:, columns] = total * scale
        copies.append(write(held, out, sems, i, (slice(None), columns)))
    for copy in copies:
        copy.wait()


def right_far(where, scale, parts, grads, done):
    owners, rows, width = parts[0].shape
    columns = grads[0].shape[1]
    blocks = max(columns // 256, PIECES)
    return written_call(
        functools.partial(right_far_kernel, blocks, scale),
        where,
        [*parts, *grads, done],
        (done.shape, F32),
        blocks,
        [pltpu.VMEM((owners * rows, CHUNKS * width), BF16)],
        2 * owners * rows * CHUNKS * width * columns,
        24,
    )


def final_kernel(scale, count, where, *refs):
    refs, (out, held, sems) = refs[:-3], refs[-3:]
    per = len(refs) // count
    width = refs[0].shape[0]
    copies = []
    for chunk in range(count):
        total = refs[chunk * per][...]
        for other in refs[chunk * per + 1 : (chunk + 1) * per]:
            total = total + other[...].astype(F32)
        rows = slice(chunk * width, (chunk + 1) * width)
        held[rows, :] = total * scale
        copies.append(write(held, out, sems, chunk, (rows, slice(None))))
    for copy in copies:
        copy.wait()


def left_final(where, scale, values, shape):
    return written_call(
        functools.partial(final_kernel, scale, CHUNKS), where, values, (shape, F32), CHUNKS, [], 0, 16
    )


def shards(activations, left_factor, right_factor, out_grad):
    groups = lax.axis_size("dp")
    width = lax.axis_size("tensor")
    tokens, depth = activations.shape
    rank = left_factor.shape[0]
    owners, peers = groups // 2, width // 2
    rows = rank // groups
    step = rows // CHUNKS
    scale = 1.0 / math.sqrt(tokens * groups)
    place, spot = lax.axis_index("tensor"), lax.axis_index("dp")
    where = jnp.stack([place % 2, place // 2, spot % 2, spot // 2, place // 2 % 2])
    where = where.astype(jnp.int32)
    run = InOrder()

    left_blocks = left_factor.reshape(owners, 2, CHUNKS, step, depth)
    right_blocks = right_factor.reshape(groups, CHUNKS, step, out_grad.shape[1])

    features = out_grad.shape[1]

    def grad_product(which, dtype, first, chunks, limit):
        return lambda *values: products(
            where,
            which,
            values,
            right_blocks,
            (groups, chunks, step, features),
            lambda i, where: (i, first, 0, 0),
            dtype,
            2,
            chunks,
            limit,
        )

    def latent_product(which, dtype):
        return lambda *values: products(
            where,
            which,
            values,
            left_blocks,
            (owners, 1, CHUNKS, step, depth),
            lambda i, where: (i, where[2], 0, 0, 0),
            dtype,
            owners,
            CHUNKS,
            24,
        )

    def halve(which, c):
        return 2 if HALVES[which][c] and peers > 1 else 1

    kept, piece, comes, near, far, latest = ({} for _ in range(6))
    theirs, left_mine, left_in = {}, {}, {}
    first_mask, masks = 2, []
    mask = 4
    while mask < width:
        masks.append(mask)
        mask *= 2

    def scoped(name, c, stage):
        return jax.named_scope(f"{NAMES[name]}{c}_{stage}")

    def grad_send(c):
        with scoped("G", c, "S"):
            (away,) = run(grad_product(0, BF16, c, 1, 24), out_grad)
            comes["G", c] = latest["G", c] = swap(away, "tensor", 1)

    def grad_keep():
        with scoped("G", "", "K"):
            for c, value in enumerate(run(grad_product(1, F32, 0, CHUNKS, 24), out_grad)):
                kept["G", c] = value

    def latent_send():
        with scoped("L", "", "S"):
            for c, value in enumerate(run(latent_product(0, BF16), *acts)):
                comes["L", c] = latest["L", c] = swap(value, "tensor", 1)

    def latent_keep():
        with scoped("L", "", "K"):
            for c, value in enumerate(run(latent_product(1, F32), *acts)):
                kept["L", c] = value

    def near_sum(name, c):
        parts = halve(name, c)
        with scoped(name, c, "near"):
            piece[name, c], away = run(
                lambda a, b: split(where, parts, a, b), kept[name, c], comes[name, c]
            )
            comes[name, c] = latest[name, c] = swap(away, "tensor", first_mask)

    def far_sum(name, c):
        for mask in masks:
            with scoped(name, c, "far"):
                piece[name, c], away = run(
                    functools.partial(added, where), piece[name, c], comes[name, c]
                )
                comes[name, c] = latest[name, c] = swap(away, "tensor", mask)

    def last_sum(name, c):
        with scoped(name, c, "last"):
            if name == "G":
                piece[name, c] = run(
                    functools.partial(summed, where), piece[name, c], comes[name, c]
                )
                forward(name, c)
            else:
                own, *others = run(
                    functools.partial(summed_by_owner, where), piece[name, c], comes[name, c]
                )
                others = [swap(v, "dp", 2 * s) for s, v in enumerate(others, 1)]
                piece[name, c], latest[name, c] = [own, *others], others

    def forward(name, c):
        if halve(name, c) == 2:
            comes[name, c] = latest[name, c] = swap(piece[name, c], "tensor", first_mask)
        else:
            spread(name, c, piece[name, c])

    def spread(name, c, value):
        near[name, c] = value
        far[name, c] = latest[name, c] = swap(value, "tensor", 1)

    def stack(name, c):
        with scoped(name, c, "stack"):
            piece[name, c] = run(functools.partial(stacked, where), *piece[name, c])
            forward(name, c)

    def join(name, c):
        if halve(name, c) == 2:
            with scoped(name, c, "join"):
                spread(
                    name, c, run(functools.partial(joined, where), piece[name, c], comes[name, c])
                )

    def core_halves(c):
        with scoped("G", c, "halves"):
            theirs[c] = latest["G", c] = swap(
                run(lambda a, b: halves(where, owners, a, b), near["G", c], far["G", c]), "dp", 1
            )

    def left(c):
        with scoped("G", c, "left"):
            left_mine[c], out = run(
                lambda *v: left_parts(where, owners, *v),
                near["G", c],
                far["G", c],
                theirs[c],
                *acts,
            )
            left_in[c] = latest["G", c] = [swap(v, "dp", 2 * s) for s, v in enumerate(out, 1)]

    def inputs():
        with scoped("G", "", "input"):
            return run(
                lambda f, *v: input_product(where, v, f, tokens),
                left_factor,
                *(v for c in range(CHUNKS) for v in [near["G", c], far["G", c]]),
            )

    def rights_near():
        with scoped("L", "", "rn"):
            return run(
                lambda *v: right_near(where, v[:CHUNKS], v[CHUNKS:]),
                *(near["L", c] for c in range(CHUNKS)),
                *grads,
            )

    def rights_far(done):
        with scoped("L", "", "rf"):
            return run(
                lambda d, *v: right_far(where, scale, v[:CHUNKS], v[CHUNKS:], d),
                done,
                *(far["L", c] for c in range(CHUNKS)),
                *grads,
            )

    def final():
        with scoped("G", "", "final"):
            return run(
                lambda *v: left_final(where, scale, v, (rows, depth)),
                *(v for c in range(CHUNKS) for v in [left_mine[c], *left_in[c]]),
            )

    def settle(*values):
        run.last = (run.last, values)

    far_grads, acts, grads = [], [activations], [out_grad]

    def far_start():
        with scoped("x", "", "og"):
            for s in range(1, owners):
                far_grads.append(swap(tied(out_grad, run), "dp", 2 * s))

    def acts_swap():
        with scoped("c", "", "acts"):
            acts.append(swap(tied(activations, run), "dp", 1))

    def own_swap():
        with scoped("c", "", "own"):
            grads.append(swap(tied(out_grad, run), "dp", 1))

    def far_swaps():
        with scoped("c", "", "far"):
            for block in far_grads:
                width = block.shape[1] // PIECES
                grads.append(block)
                for i in range(PIECES):
                    grads.append(swap(block[:, i * width : (i + 1) * width], "dp", 1))
    input_grad = right_grad = left_grad = None
    actions = {
        "near": near_sum,
        "far": far_sum,
        "last": last_sum,
        "join": join,
        "stack": stack,
    }
    for entry in ORDER:
        run.free = entry[0] == "~"
        entry = entry.lstrip("~")
        if entry == "GK":
            grad_keep()
        elif entry == "LS":
            latent_send()
        elif entry == "LK":
            latent_keep()
        elif entry == "Lrn":
            right_near_sum = rights_near()
        elif entry == "Lrf":
            right_grad = rights_far(right_near_sum)
        elif entry == "input":
            input_grad = inputs()
        elif entry == "final":
            left_grad = final()
        elif entry == "own":
            own_swap()
        elif entry == "acts":
            acts_swap()
        elif entry == "far":
            far_start()
        elif entry == "@own":
            settle(grads[1])
        elif entry == "og":
            far_swaps()
        elif entry == "@og":
            settle(*grads)
        elif entry[0] == "@":
            settle(latest[entry[1], int(entry[2])])
        else:
            name, c, stage = entry[0], int(entry[1]), entry[2:]
            if stage == "S":
                grad_send(c)
            elif stage == "halves":
                core_halves(c)
            elif stage == "left":
                left(c)
            else:
                actions[stage](name, c)
    return input_grad, left_grad, right_grad


def solution(mesh):
    placed = (P("dp", "tensor"), P(None, "tensor"), P(None, "tensor"), P("dp", "tensor"))
    return jax.shard_map(
        shards,
        mesh=mesh,
        in_specs=placed,
        out_specs=(P("dp", "tensor"), P("dp", "tensor"), P("dp", "tensor")),
        check_vma=False,
    )
```

```python
import functools
import math

import jax
import jax.numpy as jnp
from jax import lax
from jax.experimental import pallas as pl
from jax.experimental.pallas import tpu as pltpu
from jax.sharding import PartitionSpec as P

CHUNKS = 2
NAMES = {"G": "latent_grad", "L": "latent", "x": "far", "c": "core"}
PIECES = 4
ORDER = (
    "own", "far", "G0S", "acts", "G1S", "GK", "LS", "@own", "LK", "G0near", "G1near", "G0far",
    "L0near", "G1far", "L1near", "G0last", "L0far", "G1last", "L1far", "G0join", "L0last",
    "G1join", "L0stack", "L1last", "G0halves", "L0join", "og", "L1stack", "G1halves", "G0left",
    "L1join", "G1left", "input", "Lrn", "Lrf", "final",
)
HALVES = {"G": (True, True), "L": (True, True)}
BF16 = jnp.bfloat16
F32 = jnp.float32
MIB = 1 << 20
COLS = (((1,), (1,)), ((), ()))
ROWS = (((0,), (0,)), ((), ()))


def dot(first, second, dims):
    return lax.dot_general(first, second, dims, preferred_element_type=F32)


def cost(flops, *arrays):
    sizes = []
    for array in arrays:
        shape, dtype = array if isinstance(array, tuple) else (array.shape, array.dtype)
        sizes.append(math.prod(shape) * jnp.dtype(dtype).itemsize)
    return pl.CostEstimate(flops=flops, bytes_accessed=sum(sizes), transcendentals=0)


def whole_call(kernel, where, values, outs, scratch=(), flops=0):
    return pl.pallas_call(
        kernel,
        out_shape=[jax.ShapeDtypeStruct(s, t) for s, t in outs],
        in_specs=[pl.BlockSpec(memory_space=pltpu.SMEM)]
        + [pl.BlockSpec(memory_space=pltpu.VMEM)] * len(values),
        out_specs=[pl.BlockSpec(memory_space=pltpu.VMEM)] * len(outs),
        scratch_shapes=list(scratch),
        compiler_params=pltpu.CompilerParams(vmem_limit_bytes=24 * MIB),
        cost_estimate=cost(flops, *values, *outs),
    )(where, *values)


def swap(value, axis, mask):
    size = lax.axis_size(axis)
    return lax.ppermute(value, axis, [(i, i ^ mask) for i in range(size)])


def tied(value, run):
    return lax.optimization_barrier((value, run.last))[0]


class InOrder:
    def __init__(self):
        self.last = ()
        self.free = False

    def __call__(self, step, *values):
        if self.free:
            return step(*values)
        values, _ = lax.optimization_barrier((values, self.last))
        result = step(*values)
        self.last = result
        return result


def product_kernel(bit, which, first, by_core, where, *refs):
    factor = next(i for i, ref in enumerate(refs) if ref.ndim > 2)
    values, factor, outs = refs[:factor], refs[factor], refs[factor + 1 :]
    count, half, width = outs[0].shape
    half //= len(values)
    low = where[bit] if which else 1 - where[bit]
    span = pl.ds(pl.multiple_of(low * half, half), half)
    chunks = slice(first, first + len(outs))
    group = 2 if len(outs) == 1 and count % 2 == 0 else 1
    for j in range(0, count, group):
        blocks = []
        for k in range(j, j + group):
            block = factor[k, where[2], chunks] if by_core else factor[k, chunks]
            blocks.append(block.reshape(len(outs) * width, block.shape[-1]))
        flat = jnp.concatenate(blocks) if group > 1 else blocks[0]
        for i, value in enumerate(values):
            result = dot(value[span, :], flat, COLS)
            for k in range(group):
                for c, out in enumerate(outs):
                    lane = (k * len(outs) + c) * width
                    part = result[:, lane : lane + width]
                    out[j + k, i * half : (i + 1) * half, :] = part.astype(out.dtype)


def products(where, bit, which, values, factor, dtype, first, chunks, by_core):
    rows, depth = values[0].shape
    count, width = factor.shape[0], factor.shape[-2]
    total = rows // 2 * len(values)
    return whole_call(
        functools.partial(product_kernel, bit, which, first, by_core),
        where,
        [*values, factor],
        [((count, total, width), dtype)] * chunks,
        (),
        2 * total * depth * count * chunks * width,
    )


def split_kernel(where, kept, sent, mine, away):
    rows = mine.shape[1]
    if rows == kept.shape[1]:
        total = kept[...] + sent[...].astype(F32)
        mine[...] = total
        away[...] = total.astype(BF16)
        return
    for out, at in ((mine, where[4]), (away, 1 - where[4])):
        span = pl.ds(pl.multiple_of(at * rows, rows), rows)
        out[...] = (kept[:, span, :] + sent[:, span, :].astype(F32)).astype(out.dtype)


def split(where, parts, kept, sent):
    count, rows, width = kept.shape
    shape = (count, rows // parts, width)
    return whole_call(split_kernel, where, [kept, sent], [(shape, F32), (shape, BF16)])


def added_kernel(where, mine, other, out, away):
    total = mine[...] + other[...].astype(F32)
    out[...] = total
    away[...] = total.astype(BF16)


def added(where, mine, other):
    return whole_call(
        added_kernel, where, [mine, other], [(mine.shape, F32), (mine.shape, BF16)]
    )


def summed_kernel(where, mine, other, out):
    out[...] = (mine[...] + other[...].astype(F32)).astype(BF16)


def summed(where, mine, other):
    return whole_call(summed_kernel, where, [mine, other], [(mine.shape, BF16)])[0]


def summed_by_owner_kernel(where, mine, other, *outs):
    for step, out in enumerate(outs):
        at = where[3] ^ step
        out[...] = (mine[at] + other[at].astype(F32)).astype(BF16)


def summed_by_owner(where, mine, other):
    owners = mine.shape[0]
    return whole_call(
        summed_by_owner_kernel, where, [mine, other], [(mine.shape[1:], BF16)] * owners
    )


def stacked_kernel(where, *refs):
    *pieces, out = refs
    for i, piece in enumerate(pieces):
        out[i] = piece[...]


def stacked(where, *pieces):
    return whole_call(
        stacked_kernel, where, list(pieces), [((len(pieces),) + pieces[0].shape, BF16)]
    )[0]


def joined_kernel(where, mine, other, out):
    rows = mine.shape[1]
    for part, at in ((mine, where[4]), (other, 1 - where[4])):
        out[:, pl.ds(pl.multiple_of(at * rows, rows), rows), :] = part[...]


def joined(where, mine, other):
    count, rows, width = mine.shape
    return whole_call(joined_kernel, where, [mine, other], [((count, 2 * rows, width), BF16)])[0]


def halves_kernel(owners, where, near, far, out):
    for i, part in enumerate((near, far)):
        for owner in range(owners):
            out[i, owner] = part[owner * 2 + 1 - where[2]]


def halves(where, owners, near, far):
    return whole_call(
        functools.partial(halves_kernel, owners),
        where,
        [near, far],
        [((2, owners) + near.shape[1:], BF16)],
    )[0]


def left_kernel(owners, where, near, far, theirs, acts, acts_other, mine, *rest):
    blocks, (ordered, result) = rest[: owners - 1], rest[owners - 1 :]
    _, share, width = near.shape
    for i, part in enumerate((near, far)):
        low = where[0] if i == 0 else 1 - where[0]
        span = pl.ds(pl.multiple_of(low * share, share), share)
        for owner in range(owners):
            lanes = slice(owner * width, (owner + 1) * width)
            ordered[0, span, lanes] = part[owner * 2 + where[2]]
            ordered[1, span, lanes] = theirs[i, owner]
    result[...] = dot(ordered[0], acts[...], ROWS) + dot(ordered[1], acts_other[...], ROWS)
    for step in range(owners):
        rows = pl.ds(pl.multiple_of((where[3] ^ step) * width, width), width)
        if step:
            blocks[step - 1][...] = result[rows, :].astype(BF16)
        else:
            mine[...] = result[rows, :]


def left_parts(where, owners, near, far, theirs, acts, acts_other):
    width = near.shape[-1]
    tokens, depth = acts.shape
    mine, *blocks = whole_call(
        functools.partial(left_kernel, owners),
        where,
        [near, far, theirs, acts, acts_other],
        [((width, depth), F32)] + [((width, depth), BF16)] * (owners - 1),
        [
            pltpu.VMEM((2, tokens, owners * width), BF16),
            pltpu.VMEM((owners * width, depth), F32),
        ],
        4 * tokens * owners * width * depth,
    )
    return mine, blocks


def written_call(kernel, where, values, out, blocks, scratch, flops, limit):
    shape, dtype = out
    return pl.pallas_call(
        kernel,
        out_shape=jax.ShapeDtypeStruct(shape, dtype),
        in_specs=[pl.BlockSpec(memory_space=pltpu.SMEM)]
        + [pl.BlockSpec(memory_space=pltpu.VMEM)] * len(values),
        out_specs=pl.BlockSpec(memory_space=pltpu.HBM),
        scratch_shapes=[
            pltpu.VMEM(shape, dtype),
            pltpu.SemaphoreType.DMA((blocks,)),
            *scratch,
        ],
        compiler_params=pltpu.CompilerParams(vmem_limit_bytes=limit * MIB),
        cost_estimate=cost(flops, *values),
    )(where, *values)


def write(held, out, sems, i, index):
    copy = pltpu.make_async_copy(held.at[index], out.at[index], sems.at[i])
    copy.start()
    return copy


def input_kernel(count, blocks, where, *refs):
    parts, (factor, out, held, sems, ordered) = refs[: 2 * count], refs[2 * count :]
    groups, share, width = parts[0].shape
    block = held.shape[1] // blocks
    for chunk in range(count):
        for i in range(2):
            low = where[0] if i == 0 else 1 - where[0]
            span = pl.ds(pl.multiple_of(low * share, share), share)
            for group in range(groups):
                lane = (group * count + chunk) * width
                ordered[span, lane : lane + width] = parts[2 * chunk + i][group]
    copies = []
    for i in range(blocks):
        columns = slice(i * block, (i + 1) * block)
        held[:, columns] = jnp.dot(
            ordered[...], factor[:, columns], preferred_element_type=F32
        ).astype(BF16)
        copies.append(write(held, out, sems, i, (slice(None), columns)))
    for copy in copies:
        copy.wait()


def input_product(where, parts, factor, tokens):
    rank, depth = factor.shape
    blocks = max(depth // 256, 1)
    return written_call(
        functools.partial(input_kernel, len(parts) // 2, blocks),
        where,
        [*parts, factor],
        ((tokens, depth), BF16),
        blocks,
        [pltpu.VMEM((tokens, rank), BF16)],
        2 * tokens * rank * depth,
        16,
    )


def right_sum(low, parts, grads, ordered, columns):
    share = parts[0].shape[1] // 2
    span = pl.ds(pl.multiple_of(low * share, share), share)
    total = None
    refs = list(grads)
    for i in range(ordered.shape[0] // share):
        pieces = [refs.pop(0) for _ in range(pieces_of(i))]
        width = pieces[0].shape[1]
        at, start = divmod(columns.start, width)
        grad = pieces[at][span, start : start + columns.stop - columns.start]
        term = dot(ordered[i * share : (i + 1) * share, :], grad, ROWS)
        total = term if total is None else total + term
    return total


def pieces_of(i):
    return PIECES if i >= 2 and i % 2 else 1


def order_parts(parts, ordered):
    width = parts[0].shape[2]
    for c, part in enumerate(parts):
        ordered[:, c * width : (c + 1) * width] = part[...].reshape(ordered.shape[0], width)


def right_near_kernel(blocks, where, *refs):
    parts, grads, (out, ordered) = refs[:CHUNKS], refs[CHUNKS:-2], refs[-2:]
    block = out.shape[1] // blocks
    order_parts(parts, ordered)
    for i in range(blocks):
        columns = slice(i * block, (i + 1) * block)
        out[:, columns] = right_sum(where[0], parts, grads, ordered, columns)


def right_near(where, parts, grads):
    owners, rows, width = parts[0].shape
    columns = grads[0].shape[1]
    return whole_call(
        functools.partial(right_near_kernel, max(columns // 512, PIECES)),
        where,
        [*parts, *grads],
        [((CHUNKS * width, columns), F32)],
        [pltpu.VMEM((owners * rows, CHUNKS * width), BF16)],
        2 * owners * rows * CHUNKS * width * columns,
    )[0]


def right_far_kernel(blocks, scale, where, *refs):
    parts, refs = refs[:CHUNKS], refs[CHUNKS:]
    grads, (done, out, held, sems, ordered) = refs[:-5], refs[-5:]
    block = held.shape[1] // blocks
    order_parts(parts, ordered)
    copies = []
    for i in range(blocks):
        columns = slice(i * block, (i + 1) * block)
        total = done[:, columns] + right_sum(1 - where[0], parts, grads, ordered, columns)
        held[:, columns] = total * scale
        copies.append(write(held, out, sems, i, (slice(None), columns)))
    for copy in copies:
        copy.wait()


def right_far(where, scale, parts, grads, done):
    owners, rows, width = parts[0].shape
    columns = grads[0].shape[1]
    blocks = max(columns // 512, PIECES)
    return written_call(
        functools.partial(right_far_kernel, blocks, scale),
        where,
        [*parts, *grads, done],
        (done.shape, F32),
        blocks,
        [pltpu.VMEM((owners * rows, CHUNKS * width), BF16)],
        2 * owners * rows * CHUNKS * width * columns,
        24,
    )


def final_kernel(scale, count, where, *refs):
    refs, (out, held, sems) = refs[:-3], refs[-3:]
    per = len(refs) // count
    width = refs[0].shape[0]
    copies = []
    for chunk in range(count):
        total = refs[chunk * per][...]
        for other in refs[chunk * per + 1 : (chunk + 1) * per]:
            total = total + other[...].astype(F32)
        rows = slice(chunk * width, (chunk + 1) * width)
        held[rows, :] = total * scale
        copies.append(write(held, out, sems, chunk, (rows, slice(None))))
    for copy in copies:
        copy.wait()


def left_final(where, scale, values, shape):
    return written_call(
        functools.partial(final_kernel, scale, CHUNKS), where, values, (shape, F32), CHUNKS, [], 0, 16
    )


def shards(activations, left_factor, right_factor, out_grad):
    groups = lax.axis_size("dp")
    width = lax.axis_size("tensor")
    tokens, depth = activations.shape
    rank = left_factor.shape[0]
    owners, peers = groups // 2, width // 2
    rows = rank // groups
    step = rows // CHUNKS
    scale = 1.0 / math.sqrt(tokens * groups)
    place, spot = lax.axis_index("tensor"), lax.axis_index("dp")
    where = jnp.stack([place % 2, place // 2, spot % 2, spot // 2, place // 2 % 2])
    where = where.astype(jnp.int32)
    run = InOrder()

    left_blocks = left_factor.reshape(owners, 2, CHUNKS, step, depth)
    right_blocks = right_factor.reshape(groups, CHUNKS, step, out_grad.shape[1])


    def grad_product(which, dtype, first, chunks):
        bit = 0
        return lambda v, f: products(where, bit, which, [v], f, dtype, first, chunks, False)

    def latent_product(which, dtype):
        bit = 0
        return lambda a, b, f: products(where, bit, which, [a, b], f, dtype, 0, CHUNKS, True)

    def halve(which, c):
        return 2 if HALVES[which][c] and peers > 1 else 1

    kept, piece, comes, near, far, latest = ({} for _ in range(6))
    theirs, left_mine, left_in = {}, {}, {}
    first_mask, masks = 2, []
    mask = 4
    while mask < width:
        masks.append(mask)
        mask *= 2

    def scoped(name, c, stage):
        return jax.named_scope(f"{NAMES[name]}{c}_{stage}")

    def grad_send(c):
        with scoped("G", c, "S"):
            (away,) = run(grad_product(0, BF16, c, 1), out_grad, right_blocks)
            comes["G", c] = latest["G", c] = swap(away, "tensor", 1)

    def grad_keep():
        with scoped("G", "", "K"):
            for c, value in enumerate(run(grad_product(1, F32, 0, CHUNKS), out_grad, right_blocks)):
                kept["G", c] = value

    def latent_send():
        with scoped("L", "", "S"):
            for c, value in enumerate(run(latent_product(0, BF16), *acts, left_blocks)):
                comes["L", c] = latest["L", c] = swap(value, "tensor", 1)

    def latent_keep():
        with scoped("L", "", "K"):
            for c, value in enumerate(run(latent_product(1, F32), *acts, left_blocks)):
                kept["L", c] = value

    def near_sum(name, c):
        parts = halve(name, c)
        with scoped(name, c, "near"):
            piece[name, c], away = run(
                lambda a, b: split(where, parts, a, b), kept[name, c], comes[name, c]
            )
            comes[name, c] = latest[name, c] = swap(away, "tensor", first_mask)

    def far_sum(name, c):
        for mask in masks:
            with scoped(name, c, "far"):
                piece[name, c], away = run(
                    functools.partial(added, where), piece[name, c], comes[name, c]
                )
                comes[name, c] = latest[name, c] = swap(away, "tensor", mask)

    def last_sum(name, c):
        with scoped(name, c, "last"):
            if name == "G":
                piece[name, c] = run(
                    functools.partial(summed, where), piece[name, c], comes[name, c]
                )
                forward(name, c)
            else:
                own, *others = run(
                    functools.partial(summed_by_owner, where), piece[name, c], comes[name, c]
                )
                others = [swap(v, "dp", 2 * s) for s, v in enumerate(others, 1)]
                piece[name, c], latest[name, c] = [own, *others], others

    def forward(name, c):
        if halve(name, c) == 2:
            comes[name, c] = latest[name, c] = swap(piece[name, c], "tensor", first_mask)
        else:
            spread(name, c, piece[name, c])

    def spread(name, c, value):
        near[name, c] = value
        far[name, c] = latest[name, c] = swap(value, "tensor", 1)

    def stack(name, c):
        with scoped(name, c, "stack"):
            piece[name, c] = run(functools.partial(stacked, where), *piece[name, c])
            forward(name, c)

    def join(name, c):
        if halve(name, c) == 2:
            with scoped(name, c, "join"):
                spread(
                    name, c, run(functools.partial(joined, where), piece[name, c], comes[name, c])
                )

    def core_halves(c):
        with scoped("G", c, "halves"):
            theirs[c] = latest["G", c] = swap(
                run(lambda a, b: halves(where, owners, a, b), near["G", c], far["G", c]), "dp", 1
            )

    def left(c):
        with scoped("G", c, "left"):
            left_mine[c], out = run(
                lambda *v: left_parts(where, owners, *v),
                near["G", c],
                far["G", c],
                theirs[c],
                *acts,
            )
            left_in[c] = latest["G", c] = [swap(v, "dp", 2 * s) for s, v in enumerate(out, 1)]

    def inputs():
        with scoped("G", "", "input"):
            return run(
                lambda f, *v: input_product(where, v, f, tokens),
                left_factor,
                *(v for c in range(CHUNKS) for v in [near["G", c], far["G", c]]),
            )

    def rights_near():
        with scoped("L", "", "rn"):
            return run(
                lambda *v: right_near(where, v[:CHUNKS], v[CHUNKS:]),
                *(near["L", c] for c in range(CHUNKS)),
                *grads,
            )

    def rights_far(done):
        with scoped("L", "", "rf"):
            return run(
                lambda d, *v: right_far(where, scale, v[:CHUNKS], v[CHUNKS:], d),
                done,
                *(far["L", c] for c in range(CHUNKS)),
                *grads,
            )

    def final():
        with scoped("G", "", "final"):
            return run(
                lambda *v: left_final(where, scale, v, (rows, depth)),
                *(v for c in range(CHUNKS) for v in [left_mine[c], *left_in[c]]),
            )

    def settle(*values):
        run.last = (run.last, values)

    far_grads, acts, grads = [], [activations], [out_grad]

    def far_start():
        with scoped("x", "", "og"):
            for s in range(1, owners):
                far_grads.append(swap(tied(out_grad, run), "dp", 2 * s))

    def acts_swap():
        with scoped("c", "", "acts"):
            acts.append(swap(tied(activations, run), "dp", 1))

    def own_swap():
        with scoped("c", "", "own"):
            grads.append(swap(tied(out_grad, run), "dp", 1))

    def far_swaps():
        with scoped("c", "", "far"):
            for block in far_grads:
                width = block.shape[1] // PIECES
                grads.append(block)
                for i in range(PIECES):
                    grads.append(swap(block[:, i * width : (i + 1) * width], "dp", 1))
    input_grad = right_grad = left_grad = None
    actions = {
        "near": near_sum,
        "far": far_sum,
        "last": last_sum,
        "join": join,
        "stack": stack,
    }
    for entry in ORDER:
        run.free = entry[0] == "~"
        entry = entry.lstrip("~")
        if entry == "GK":
            grad_keep()
        elif entry == "LS":
            latent_send()
        elif entry == "LK":
            latent_keep()
        elif entry == "Lrn":
            right_near_sum = rights_near()
        elif entry == "Lrf":
            right_grad = rights_far(right_near_sum)
        elif entry == "input":
            input_grad = inputs()
        elif entry == "final":
            left_grad = final()
        elif entry == "own":
            own_swap()
        elif entry == "acts":
            acts_swap()
        elif entry == "far":
            far_start()
        elif entry == "@own":
            settle(grads[1])
        elif entry == "og":
            far_swaps()
        elif entry == "@og":
            settle(*grads)
        elif entry[0] == "@":
            settle(latest[entry[1], int(entry[2])])
        else:
            name, c, stage = entry[0], int(entry[1]), entry[2:]
            if stage == "S":
                grad_send(c)
            elif stage == "halves":
                core_halves(c)
            elif stage == "left":
                left(c)
            else:
                actions[stage](name, c)
    return input_grad, left_grad, right_grad


def solution(mesh):
    placed = (P("dp", "tensor"), P(None, "tensor"), P(None, "tensor"), P("dp", "tensor"))
    return jax.shard_map(
        shards,
        mesh=mesh,
        in_specs=placed,
        out_specs=(P("dp", "tensor"), P("dp", "tensor"), P("dp", "tensor")),
        check_vma=False,
    )
```

```python
import functools
import math

import jax
import jax.numpy as jnp
from jax import lax
from jax.experimental import pallas as pl
from jax.experimental.pallas import tpu as pltpu
from jax.sharding import PartitionSpec as P

CHUNKS = 2
NAMES = {"G": "latent_grad", "L": "latent", "x": "far", "c": "core"}
PIECES = 4
ORDER = (
    "own", "far", "G0S", "acts", "G1S", "GK", "LS", "@own", "LK", "G0near", "G1near", "G0far",
    "L0near", "G1far", "L1near", "G0last", "L0far", "G1last", "L1far", "G0join", "L0last",
    "G1join", "L0stack", "L1last", "G0halves", "L0join", "og", "L1stack", "G1halves", "G0left",
    "L1join", "G1left", "input", "Lrn", "Lrf", "final",
)
HALVES = {"G": (True, True), "L": (True, True)}
BF16 = jnp.bfloat16
F32 = jnp.float32
MIB = 1 << 20
COLS = (((1,), (1,)), ((), ()))
ROWS = (((0,), (0,)), ((), ()))


def dot(first, second, dims):
    return lax.dot_general(first, second, dims, preferred_element_type=F32)


def cost(flops, *arrays):
    sizes = []
    for array in arrays:
        shape, dtype = array if isinstance(array, tuple) else (array.shape, array.dtype)
        sizes.append(math.prod(shape) * jnp.dtype(dtype).itemsize)
    return pl.CostEstimate(flops=flops, bytes_accessed=sum(sizes), transcendentals=0)


def whole_call(kernel, where, values, outs, scratch=(), flops=0):
    return pl.pallas_call(
        kernel,
        out_shape=[jax.ShapeDtypeStruct(s, t) for s, t in outs],
        in_specs=[pl.BlockSpec(memory_space=pltpu.SMEM)]
        + [pl.BlockSpec(memory_space=pltpu.VMEM)] * len(values),
        out_specs=[pl.BlockSpec(memory_space=pltpu.VMEM)] * len(outs),
        scratch_shapes=list(scratch),
        compiler_params=pltpu.CompilerParams(vmem_limit_bytes=24 * MIB),
        cost_estimate=cost(flops, *values, *outs),
    )(where, *values)


def swap(value, axis, mask):
    size = lax.axis_size(axis)
    return lax.ppermute(value, axis, [(i, i ^ mask) for i in range(size)])


def tied(value, run):
    return lax.optimization_barrier((value, run.last))[0]


class InOrder:
    def __init__(self):
        self.last = ()
        self.free = False

    def __call__(self, step, *values):
        if self.free:
            return step(*values)
        values, _ = lax.optimization_barrier((values, self.last))
        result = step(*values)
        self.last = result
        return result


def product_kernel(bit, which, first, by_core, where, *refs):
    factor = next(i for i, ref in enumerate(refs) if ref.ndim > 2)
    values, factor, outs = refs[:factor], refs[factor], refs[factor + 1 :]
    count, half, width = outs[0].shape
    half //= len(values)
    low = where[bit] if which else 1 - where[bit]
    span = pl.ds(pl.multiple_of(low * half, half), half)
    chunks = slice(first, first + len(outs))
    group = 2 if len(outs) == 1 and count % 2 == 0 else 1
    for j in range(0, count, group):
        blocks = []
        for k in range(j, j + group):
            block = factor[k, where[2], chunks] if by_core else factor[k, chunks]
            blocks.append(block.reshape(len(outs) * width, block.shape[-1]))
        flat = jnp.concatenate(blocks) if group > 1 else blocks[0]
        for i, value in enumerate(values):
            result = dot(value[span, :], flat, COLS)
            for k in range(group):
                for c, out in enumerate(outs):
                    lane = (k * len(outs) + c) * width
                    part = result[:, lane : lane + width]
                    out[j + k, i * half : (i + 1) * half, :] = part.astype(out.dtype)


def products(where, bit, which, values, factor, dtype, first, chunks, by_core):
    rows, depth = values[0].shape
    count, width = factor.shape[0], factor.shape[-2]
    total = rows // 2 * len(values)
    return whole_call(
        functools.partial(product_kernel, bit, which, first, by_core),
        where,
        [*values, factor],
        [((count, total, width), dtype)] * chunks,
        (),
        2 * total * depth * count * chunks * width,
    )


def split_kernel(where, kept, sent, mine, away):
    rows = mine.shape[1]
    if rows == kept.shape[1]:
        total = kept[...] + sent[...].astype(F32)
        mine[...] = total
        away[...] = total.astype(BF16)
        return
    for out, at in ((mine, where[4]), (away, 1 - where[4])):
        span = pl.ds(pl.multiple_of(at * rows, rows), rows)
        out[...] = (kept[:, span, :] + sent[:, span, :].astype(F32)).astype(out.dtype)


def split(where, parts, kept, sent):
    count, rows, width = kept.shape
    shape = (count, rows // parts, width)
    return whole_call(split_kernel, where, [kept, sent], [(shape, F32), (shape, BF16)])


def added_kernel(where, mine, other, out, away):
    total = mine[...] + other[...].astype(F32)
    out[...] = total
    away[...] = total.astype(BF16)


def added(where, mine, other):
    return whole_call(
        added_kernel, where, [mine, other], [(mine.shape, F32), (mine.shape, BF16)]
    )


def summed_kernel(where, mine, other, out):
    out[...] = (mine[...] + other[...].astype(F32)).astype(BF16)


def summed(where, mine, other):
    return whole_call(summed_kernel, where, [mine, other], [(mine.shape, BF16)])[0]


def summed_by_owner_kernel(where, mine, other, *outs):
    for step, out in enumerate(outs):
        at = where[3] ^ step
        out[...] = (mine[at] + other[at].astype(F32)).astype(BF16)


def summed_by_owner(where, mine, other):
    owners = mine.shape[0]
    return whole_call(
        summed_by_owner_kernel, where, [mine, other], [(mine.shape[1:], BF16)] * owners
    )


def stacked_kernel(where, *refs):
    *pieces, out = refs
    for i, piece in enumerate(pieces):
        out[i] = piece[...]


def stacked(where, *pieces):
    return whole_call(
        stacked_kernel, where, list(pieces), [((len(pieces),) + pieces[0].shape, BF16)]
    )[0]


def joined_kernel(where, mine, other, out):
    rows = mine.shape[1]
    for part, at in ((mine, where[4]), (other, 1 - where[4])):
        out[:, pl.ds(pl.multiple_of(at * rows, rows), rows), :] = part[...]


def joined(where, mine, other):
    count, rows, width = mine.shape
    return whole_call(joined_kernel, where, [mine, other], [((count, 2 * rows, width), BF16)])[0]


def halves_kernel(owners, where, near, far, out):
    for i, part in enumerate((near, far)):
        for owner in range(owners):
            out[i, owner] = part[owner * 2 + 1 - where[2]]


def halves(where, owners, near, far):
    return whole_call(
        functools.partial(halves_kernel, owners),
        where,
        [near, far],
        [((2, owners) + near.shape[1:], BF16)],
    )[0]


def left_kernel(owners, where, near, far, theirs, acts, acts_other, mine, *rest):
    blocks, (ordered, result) = rest[: owners - 1], rest[owners - 1 :]
    _, share, width = near.shape
    for i, part in enumerate((near, far)):
        low = where[0] if i == 0 else 1 - where[0]
        span = pl.ds(pl.multiple_of(low * share, share), share)
        for owner in range(owners):
            lanes = slice(owner * width, (owner + 1) * width)
            ordered[0, span, lanes] = part[owner * 2 + where[2]]
            ordered[1, span, lanes] = theirs[i, owner]
    result[...] = dot(ordered[0], acts[...], ROWS) + dot(ordered[1], acts_other[...], ROWS)
    for step in range(owners):
        rows = pl.ds(pl.multiple_of((where[3] ^ step) * width, width), width)
        if step:
            blocks[step - 1][...] = result[rows, :].astype(BF16)
        else:
            mine[...] = result[rows, :]


def left_parts(where, owners, near, far, theirs, acts, acts_other):
    width = near.shape[-1]
    tokens, depth = acts.shape
    mine, *blocks = whole_call(
        functools.partial(left_kernel, owners),
        where,
        [near, far, theirs, acts, acts_other],
        [((width, depth), F32)] + [((width, depth), BF16)] * (owners - 1),
        [
            pltpu.VMEM((2, tokens, owners * width), BF16),
            pltpu.VMEM((owners * width, depth), F32),
        ],
        4 * tokens * owners * width * depth,
    )
    return mine, blocks


def written_call(kernel, where, values, out, blocks, scratch, flops, limit):
    shape, dtype = out
    return pl.pallas_call(
        kernel,
        out_shape=jax.ShapeDtypeStruct(shape, dtype),
        in_specs=[pl.BlockSpec(memory_space=pltpu.SMEM)]
        + [pl.BlockSpec(memory_space=pltpu.VMEM)] * len(values),
        out_specs=pl.BlockSpec(memory_space=pltpu.HBM),
        scratch_shapes=[
            pltpu.VMEM(shape, dtype),
            pltpu.SemaphoreType.DMA((blocks,)),
            *scratch,
        ],
        compiler_params=pltpu.CompilerParams(vmem_limit_bytes=limit * MIB),
        cost_estimate=cost(flops, *values),
    )(where, *values)


def write(held, out, sems, i, index):
    copy = pltpu.make_async_copy(held.at[index], out.at[index], sems.at[i])
    copy.start()
    return copy


def input_kernel(count, blocks, where, *refs):
    parts, (factor, out, held, sems, ordered) = refs[: 2 * count], refs[2 * count :]
    groups, share, width = parts[0].shape
    block = held.shape[1] // blocks
    for chunk in range(count):
        for i in range(2):
            low = where[0] if i == 0 else 1 - where[0]
            span = pl.ds(pl.multiple_of(low * share, share), share)
            for group in range(groups):
                lane = (group * count + chunk) * width
                ordered[span, lane : lane + width] = parts[2 * chunk + i][group]
    copies = []
    for i in range(blocks):
        columns = slice(i * block, (i + 1) * block)
        held[:, columns] = jnp.dot(
            ordered[...], factor[:, columns], preferred_element_type=F32
        ).astype(BF16)
        copies.append(write(held, out, sems, i, (slice(None), columns)))
    for copy in copies:
        copy.wait()


def input_product(where, parts, factor, tokens):
    rank, depth = factor.shape
    blocks = max(depth // 256, 1)
    return written_call(
        functools.partial(input_kernel, len(parts) // 2, blocks),
        where,
        [*parts, factor],
        ((tokens, depth), BF16),
        blocks,
        [pltpu.VMEM((tokens, rank), BF16)],
        2 * tokens * rank * depth,
        16,
    )


def right_sum(low, parts, grads, ordered, columns):
    share = parts[0].shape[1] // 2
    span = pl.ds(pl.multiple_of(low * share, share), share)
    total = None
    refs = list(grads)
    for i in range(ordered.shape[0] // share):
        pieces = [refs.pop(0) for _ in range(pieces_of(i))]
        width = pieces[0].shape[1]
        at, start = divmod(columns.start, width)
        grad = pieces[at][span, start : start + columns.stop - columns.start]
        term = dot(ordered[i * share : (i + 1) * share, :], grad, ROWS)
        total = term if total is None else total + term
    return total


def pieces_of(i):
    return PIECES if i >= 2 and i % 2 else 1


def order_parts(parts, ordered):
    width = parts[0].shape[2]
    for c, part in enumerate(parts):
        ordered[:, c * width : (c + 1) * width] = part[...].reshape(ordered.shape[0], width)


def right_near_kernel(blocks, where, *refs):
    parts, grads, (out, ordered) = refs[:CHUNKS], refs[CHUNKS:-2], refs[-2:]
    block = out.shape[1] // blocks
    order_parts(parts, ordered)
    for i in range(blocks):
        columns = slice(i * block, (i + 1) * block)
        out[:, columns] = right_sum(where[0], parts, grads, ordered, columns)


def right_near(where, parts, grads):
    owners, rows, width = parts[0].shape
    columns = grads[0].shape[1]
    return whole_call(
        functools.partial(right_near_kernel, max(columns // 512, PIECES)),
        where,
        [*parts, *grads],
        [((CHUNKS * width, columns), F32)],
        [pltpu.VMEM((owners * rows, CHUNKS * width), BF16)],
        2 * owners * rows * CHUNKS * width * columns,
    )[0]


def right_far_kernel(blocks, scale, where, *refs):
    parts, refs = refs[:CHUNKS], refs[CHUNKS:]
    grads, (done, out, held, sems, ordered) = refs[:-5], refs[-5:]
    block = held.shape[1] // blocks
    order_parts(parts, ordered)
    copies = []
    for i in range(blocks):
        columns = slice(i * block, (i + 1) * block)
        total = done[:, columns] + right_sum(1 - where[0], parts, grads, ordered, columns)
        held[:, columns] = total * scale
        copies.append(write(held, out, sems, i, (slice(None), columns)))
    for copy in copies:
        copy.wait()


def right_far(where, scale, parts, grads, done):
    owners, rows, width = parts[0].shape
    columns = grads[0].shape[1]
    blocks = max(columns // 512, PIECES)
    return written_call(
        functools.partial(right_far_kernel, blocks, scale),
        where,
        [*parts, *grads, done],
        (done.shape, F32),
        blocks,
        [pltpu.VMEM((owners * rows, CHUNKS * width), BF16)],
        2 * owners * rows * CHUNKS * width * columns,
        24,
    )


def final_kernel(scale, count, blocks, where, *refs):
    refs, (out, held, sems) = refs[:-3], refs[-3:]
    per = len(refs) // count
    width = refs[0].shape[0]
    rows = width // blocks
    copies = []
    for chunk in range(count):
        for i in range(blocks):
            part = slice(i * rows, (i + 1) * rows)
            total = refs[chunk * per][part, :]
            for other in refs[chunk * per + 1 : (chunk + 1) * per]:
                total = total + other[part, :].astype(F32)
            span = slice(chunk * width + i * rows, chunk * width + (i + 1) * rows)
            held[span, :] = total * scale
            copies.append(write(held, out, sems, chunk * blocks + i, (span, slice(None))))
    for copy in copies:
        copy.wait()


def left_final(where, scale, values, shape):
    return written_call(
        functools.partial(final_kernel, scale, CHUNKS, 2),
        where,
        values,
        (shape, F32),
        2 * CHUNKS,
        [],
        0,
        16,
    )


def shards(activations, left_factor, right_factor, out_grad):
    groups = lax.axis_size("dp")
    width = lax.axis_size("tensor")
    tokens, depth = activations.shape
    rank = left_factor.shape[0]
    owners, peers = groups // 2, width // 2
    rows = rank // groups
    step = rows // CHUNKS
    scale = 1.0 / math.sqrt(tokens * groups)
    place, spot = lax.axis_index("tensor"), lax.axis_index("dp")
    where = jnp.stack([place % 2, place // 2, spot % 2, spot // 2, place // 2 % 2])
    where = where.astype(jnp.int32)
    run = InOrder()

    left_blocks = left_factor.reshape(owners, 2, CHUNKS, step, depth)
    right_blocks = right_factor.reshape(groups, CHUNKS, step, out_grad.shape[1])


    def grad_product(which, dtype, first, chunks):
        bit = 0
        return lambda v, f: products(where, bit, which, [v], f, dtype, first, chunks, False)

    def latent_product(which, dtype):
        bit = 0
        return lambda a, b, f: products(where, bit, which, [a, b], f, dtype, 0, CHUNKS, True)

    def halve(which, c):
        return 2 if HALVES[which][c] and peers > 1 else 1

    kept, piece, comes, near, far, latest = ({} for _ in range(6))
    theirs, left_mine, left_in = {}, {}, {}
    first_mask, masks = 2, []
    mask = 4
    while mask < width:
        masks.append(mask)
        mask *= 2

    def scoped(name, c, stage):
        return jax.named_scope(f"{NAMES[name]}{c}_{stage}")

    def grad_send(c):
        with scoped("G", c, "S"):
            (away,) = run(grad_product(0, BF16, c, 1), out_grad, right_blocks)
            comes["G", c] = latest["G", c] = swap(away, "tensor", 1)

    def grad_keep():
        with scoped("G", "", "K"):
            for c, value in enumerate(run(grad_product(1, F32, 0, CHUNKS), out_grad, right_blocks)):
                kept["G", c] = value

    def latent_send():
        with scoped("L", "", "S"):
            for c, value in enumerate(run(latent_product(0, BF16), *acts, left_blocks)):
                comes["L", c] = latest["L", c] = swap(value, "tensor", 1)

    def latent_keep():
        with scoped("L", "", "K"):
            for c, value in enumerate(run(latent_product(1, F32), *acts, left_blocks)):
                kept["L", c] = value

    def near_sum(name, c):
        parts = halve(name, c)
        with scoped(name, c, "near"):
            piece[name, c], away = run(
                lambda a, b: split(where, parts, a, b), kept[name, c], comes[name, c]
            )
            comes[name, c] = latest[name, c] = swap(away, "tensor", first_mask)

    def far_sum(name, c):
        for mask in masks:
            with scoped(name, c, "far"):
                piece[name, c], away = run(
                    functools.partial(added, where), piece[name, c], comes[name, c]
                )
                comes[name, c] = latest[name, c] = swap(away, "tensor", mask)

    def last_sum(name, c):
        with scoped(name, c, "last"):
            if name == "G":
                piece[name, c] = run(
                    functools.partial(summed, where), piece[name, c], comes[name, c]
                )
                forward(name, c)
            else:
                own, *others = run(
                    functools.partial(summed_by_owner, where), piece[name, c], comes[name, c]
                )
                others = [swap(v, "dp", 2 * s) for s, v in enumerate(others, 1)]
                piece[name, c], latest[name, c] = [own, *others], others

    def forward(name, c):
        if halve(name, c) == 2:
            comes[name, c] = latest[name, c] = swap(piece[name, c], "tensor", first_mask)
        else:
            spread(name, c, piece[name, c])

    def spread(name, c, value):
        near[name, c] = value
        far[name, c] = latest[name, c] = swap(value, "tensor", 1)

    def stack(name, c):
        with scoped(name, c, "stack"):
            piece[name, c] = run(functools.partial(stacked, where), *piece[name, c])
            forward(name, c)

    def join(name, c):
        if halve(name, c) == 2:
            with scoped(name, c, "join"):
                spread(
                    name, c, run(functools.partial(joined, where), piece[name, c], comes[name, c])
                )

    def core_halves(c):
        with scoped("G", c, "halves"):
            theirs[c] = latest["G", c] = swap(
                run(lambda a, b: halves(where, owners, a, b), near["G", c], far["G", c]), "dp", 1
            )

    def left(c):
        with scoped("G", c, "left"):
            left_mine[c], out = run(
                lambda *v: left_parts(where, owners, *v),
                near["G", c],
                far["G", c],
                theirs[c],
                *acts,
            )
            left_in[c] = latest["G", c] = [swap(v, "dp", 2 * s) for s, v in enumerate(out, 1)]

    def inputs():
        with scoped("G", "", "input"):
            return run(
                lambda f, *v: input_product(where, v, f, tokens),
                left_factor,
                *(v for c in range(CHUNKS) for v in [near["G", c], far["G", c]]),
            )

    def rights_near():
        with scoped("L", "", "rn"):
            return run(
                lambda *v: right_near(where, v[:CHUNKS], v[CHUNKS:]),
                *(near["L", c] for c in range(CHUNKS)),
                *grads,
            )

    def rights_far(done):
        with scoped("L", "", "rf"):
            return run(
                lambda d, *v: right_far(where, scale, v[:CHUNKS], v[CHUNKS:], d),
                done,
                *(far["L", c] for c in range(CHUNKS)),
                *grads,
            )

    def final():
        with scoped("G", "", "final"):
            return run(
                lambda *v: left_final(where, scale, v, (rows, depth)),
                *(v for c in range(CHUNKS) for v in [left_mine[c], *left_in[c]]),
            )

    def settle(*values):
        run.last = (run.last, values)

    far_grads, acts, grads = [], [activations], [out_grad]

    def far_start():
        with scoped("x", "", "og"):
            for s in range(1, owners):
                far_grads.append(swap(tied(out_grad, run), "dp", 2 * s))

    def acts_swap():
        with scoped("c", "", "acts"):
            acts.append(swap(tied(activations, run), "dp", 1))

    def own_swap():
        with scoped("c", "", "own"):
            grads.append(swap(tied(out_grad, run), "dp", 1))

    def far_swaps():
        with scoped("c", "", "far"):
            for block in far_grads:
                width = block.shape[1] // PIECES
                grads.append(block)
                for i in range(PIECES):
                    grads.append(swap(block[:, i * width : (i + 1) * width], "dp", 1))
    input_grad = right_grad = left_grad = None
    actions = {
        "near": near_sum,
        "far": far_sum,
        "last": last_sum,
        "join": join,
        "stack": stack,
    }
    for entry in ORDER:
        run.free = entry[0] == "~"
        entry = entry.lstrip("~")
        if entry == "GK":
            grad_keep()
        elif entry == "LS":
            latent_send()
        elif entry == "LK":
            latent_keep()
        elif entry == "Lrn":
            right_near_sum = rights_near()
        elif entry == "Lrf":
            right_grad = rights_far(right_near_sum)
        elif entry == "input":
            input_grad = inputs()
        elif entry == "final":
            left_grad = final()
        elif entry == "own":
            own_swap()
        elif entry == "acts":
            acts_swap()
        elif entry == "far":
            far_start()
        elif entry == "@own":
            settle(grads[1])
        elif entry == "og":
            far_swaps()
        elif entry == "@og":
            settle(*grads)
        elif entry[0] == "@":
            settle(latest[entry[1], int(entry[2])])
        else:
            name, c, stage = entry[0], int(entry[1]), entry[2:]
            if stage == "S":
                grad_send(c)
            elif stage == "halves":
                core_halves(c)
            elif stage == "left":
                left(c)
            else:
                actions[stage](name, c)
    return input_grad, left_grad, right_grad


def solution(mesh):
    placed = (P("dp", "tensor"), P(None, "tensor"), P(None, "tensor"), P("dp", "tensor"))
    return jax.shard_map(
        shards,
        mesh=mesh,
        in_specs=placed,
        out_specs=(P("dp", "tensor"), P("dp", "tensor"), P("dp", "tensor")),
        check_vma=False,
    )
```
